32 devices in a mesh: groups: 1, gx: 8 (over z, y), gy: 2 (over core), segment: 2 (over x).
Axes of the slice: x: 2, y: 2, z: 4, core: 2. Of those that a mesh axis runs over, the one named last changes fastest.
Arguments:
- activations: bfloat16 [2, 8, 128, 128, 128], P('segment', 'groups', 'gx', 'gy'), may hold values from -6 to 6
- cotangent: bfloat16 [8, 128, 128, 128], P('groups', 'gx', 'gy'), may hold values from -6 to 6
- spectral_weights: float32 [2, 32, 32, 8, 8, 32], P('segment', 'gy', 'gx'), may hold values from -6 to 6
- pointwise: float32 [2, 8, 8], P('segment'), may hold values from -2 to 2
- channel_bias: float32 [2, 8], P('segment'), may hold values from -3 to 3
Outputs:
- input_grads: bfloat16 [2, 8, 128, 128, 128], P('segment', 'groups', 'gx', 'gy')
- spectral_grads: float32 [2, 32, 32, 8, 8, 32], P('segment', 'gy', 'gx', 'groups')
The draws below stay inside these ranges and needn't reach their ends.
All inputs are finite; a program needn't handle non-finite values.
Results may differ from the reference program's by a relative error of at most 0.0042.
Values may be sent and summed in bfloat16 or wider, within the bound.
No kernel may reach another device: no remote copies, remote signals or barrier semaphores. Data moves between devices by JAX's collectives and lax.ppermute only.
A program may use at most 64 MiB of HBM per device.

```python
import math
import jax
import jax.numpy as jnp
from jax import lax

C = 8
NX = 128
NY = 128
NZ = 128
MODES = 32
SEGMENTS = 2


def levels(key, extent, split, low, high):
    loudness, own = 1.0, jax.random.fold_in(key, 6)
    for axis_at, shards_of in split:
        heights = jnp.exp(jax.random.uniform(jax.random.fold_in(own, axis_at), (shards_of,), jnp.float32, low / len(split), high / len(split)))
        loudness = loudness * jnp.repeat(heights, extent[axis_at] // shards_of).reshape([-1 if axis == axis_at else 1 for axis in range(len(extent))])
    return loudness


def scatter_about(own_key, extent, spread, most, pieces=(), kind=jnp.bfloat16):
    level = levels(own_key, extent, pieces, -0.22, 0.18) if pieces else 1.0
    result = jax.random.normal(own_key, extent, jnp.float32) * spread * level
    return jnp.minimum(jnp.maximum(result, -most), most).astype(kind)


def setup_inputs(seed: int = 0, part: int = 0) -> dict:
    arg_keys = jax.random.split(jax.random.key(seed), 6)
    own_keys = jax.random.split(jax.random.fold_in(arg_keys[5], part), 6)
    activations = scatter_about(own_keys[0], (SEGMENTS, C, NX, NY, NZ), 1.0, 6.0, ((0, 2), (2, 8), (3, 2)))
    cotangent = scatter_about(own_keys[1], (C, NX, NY, NZ), 1.0, 6.0, ((1, 8), (2, 2)))
    spectral_weights = scatter_about(arg_keys[2], (SEGMENTS, MODES, MODES, C, C, MODES), 1.0, 6.0, ((0, 2), (1, 2), (2, 8)), jnp.float32)
    pointwise = scatter_about(arg_keys[3], (SEGMENTS, C, C), C ** -0.5, 2.0, ((0, 2),), jnp.float32)
    channel_bias = scatter_about(arg_keys[4], (SEGMENTS, C), 0.7, 3.0, ((0, 2),), jnp.float32)
    return dict(activations=activations, cotangent=cotangent, spectral_weights=spectral_weights, pointwise=pointwise, channel_bias=channel_bias)


highest = lax.Precision.HIGHEST

def trig_basis(length, mode_count):
    half = mode_count // 2
    freqs = jnp.arange(half, dtype=jnp.int32)[:, None]
    points = jnp.arange(length, dtype=jnp.int32)[None, :]
    step_angle = 2.0 * math.pi / length
    cosine = jnp.cos((freqs * points % length).astype(jnp.float32) * step_angle)
    sine = jnp.sin(((freqs + 1) * points % length).astype(jnp.float32) * step_angle)
    rows_all = jnp.concatenate([cosine, sine], axis=0)
    scales = jnp.where(jnp.arange(mode_count) == 0, 1.0 / math.sqrt(length), math.sqrt(2.0 / length)).astype(jnp.float32)
    return rows_all * scales[:, None]

def to_modes(field, along_x, along_y, along_z):
    inner = jnp.einsum('ixyz,cz->cixy', field, along_z, precision=highest)
    inner = jnp.einsum('cixy,ax->ciay', inner, along_x, precision=highest)
    return jnp.einsum('ciay,jy->jcia', inner, along_y, precision=highest)

def to_field(spectrum, along_x, along_y, along_z):
    inner = jnp.einsum('jcia,jy->ciay', spectrum, along_y, precision=highest)
    inner = jnp.einsum('ciay,ax->cixy', inner, along_x, precision=highest)
    return jnp.einsum('cixy,cz->ixyz', inner, along_z, precision=highest)

def gelu_slope(value):
    normal_cdf = 0.5 * (1.0 + jax.scipy.special.erf(value * 0.7071067811865476))
    return normal_cdf + value * jnp.exp(-0.5 * value * value) * 0.3989422804014327

def reference(activations, cotangent, spectral_weights, pointwise, channel_bias):
    along_x = trig_basis(NX, MODES)
    along_y = trig_basis(NY, MODES)
    along_z = trig_basis(NZ, MODES)
    incoming = cotangent
    grad_fields = []
    weight_grads = []
    for segment_index in range(SEGMENTS - 1, -1, -1):
        inputs = activations[segment_index].astype(jnp.float32)
        weights = spectral_weights[segment_index]
        mixing = pointwise[segment_index]
        input_modes = to_modes(inputs, along_x, along_y, along_z)
        mixed = jnp.einsum('jcioa,jcia->jcoa', weights, input_modes, precision=highest)
        pre_act = jnp.einsum('oi,ixyz->oxyz', mixing, inputs, precision=highest)
        pre_act = pre_act + channel_bias[segment_index][:, None, None, None] + to_field(mixed, along_x, along_y, along_z)
        signal = incoming.astype(jnp.float32) * gelu_slope(pre_act)
        grad_modes = to_modes(signal, along_x, along_y, along_z)
        back = jnp.einsum('jcioa,jcoa->jcia', weights, grad_modes, precision=highest)
        input_grad = jnp.einsum('oi,oxyz->ixyz', mixing, signal, precision=highest) + to_field(back, along_x, along_y, along_z)
        input_grad = input_grad.astype(jnp.bfloat16)
        grad_fields.append(input_grad)
        weight_grads.append(jnp.einsum('jcia,jcoa->jcioa', input_modes, grad_modes, precision=highest))
        incoming = input_grad
    ordered_fields = grad_fields[::-1]
    ordered_weights = weight_grads[::-1]
    return (jnp.stack(ordered_fields), jnp.stack(ordered_weights))
```

```python
import functools
import math

import jax
import jax.numpy as jnp
import ml_dtypes
import numpy as np
from jax import lax
from jax.experimental import pallas as pl
from jax.experimental.pallas import tpu as pltpu
from jax.sharding import PartitionSpec as P

MODES = 32
LANES = 128
PLANE = ("gx", "gy")
F32 = jnp.float32
BF16 = jnp.bfloat16
VMEM_LIMIT = 40 * 1024 * 1024


def trig_basis(length):
    half = MODES // 2
    points = np.arange(length)[None, :]
    freqs = np.arange(half)[:, None]
    angle = 2.0 * math.pi / length
    rows = np.concatenate(
        [np.cos((freqs * points % length) * angle), np.sin(((freqs + 1) * points % length) * angle)], axis=0
    )
    scales = np.where(np.arange(MODES) == 0, 1.0 / math.sqrt(length), math.sqrt(2.0 / length))
    return rows * scales[:, None]


def high_low(values):
    high = values.astype(np.float32).astype(ml_dtypes.bfloat16)
    low = (values - high.astype(np.float64)).astype(np.float32).astype(ml_dtypes.bfloat16)
    return np.stack([high, low])


class Plan:
    def __init__(self, channels, rows_x, rows_y, length_z, count_x, count_y):
        self.channels, self.rows_x, self.rows_y, self.length_z = channels, rows_x, rows_y, length_z
        self.count_x, self.count_y = count_x, count_y
        self.devices = count_x * count_y
        self.padded_x = -(-rows_x // 16) * 16
        self.block_x = math.gcd(rows_x, 4)
        self.blocks = rows_x // self.block_x
        self.rows = self.block_x * rows_y
        self.own_third = MODES // count_x
        self.own_second = MODES // count_y
        self.width = self.own_third * channels
        self.per_tile = LANES // self.width
        self.tiles = self.own_second // self.per_tile
        self.halves = MODES * channels // LANES
        self.wire = (self.devices, self.padded_x, self.own_second * self.width)
        self.pairs = self.own_second * self.own_third
        along_x = trig_basis(rows_x * count_x)
        along_y = trig_basis(rows_y * count_y)
        along_z = trig_basis(length_z)
        third = np.einsum("ik,cz->izck", np.eye(channels), along_z)
        third = third.reshape(channels * length_z, MODES * channels)
        self.third = high_low(third)
        self.third_t = high_low(third.T)
        slabs = along_y.reshape(MODES, count_y, rows_y)
        pick = np.zeros((self.padded_x, self.blocks, self.block_x))
        for x in range(rows_x):
            pick[x, x // self.block_x, x % self.block_x] = 1.0
        second = np.einsum("jhy,xbk->hbjxky", slabs, pick)
        second = second.reshape(count_y, self.blocks, MODES * self.padded_x, self.rows)
        self.second = np.moveaxis(high_low(second), 0, 2)
        self.second_t = np.moveaxis(high_low(np.swapaxes(second, 2, 3)), 0, 2)
        padded = np.zeros((MODES, count_x, self.padded_x))
        padded[:, :, :rows_x] = along_x.reshape(MODES, count_x, rows_x)
        first = np.repeat(padded[:, :, None, :], count_y, axis=2)
        self.first = high_low(first.reshape(MODES, self.devices * self.padded_x))
        self.first_t = high_low(padded.reshape(MODES, count_x * self.padded_x).T)


def dot(a, b):
    return jnp.dot(a, b, preferred_element_type=F32)


def split(value):
    high = value.astype(BF16)
    return high, (value - high.astype(F32)).astype(BF16)


def swap_groups(parts, width):
    parts = list(parts)
    lane = lax.broadcasted_iota(jnp.int32, parts[0].shape, 1)
    bit = len(parts) // 2
    while bit:
        shift = bit * width
        low = (lane // shift) % 2 == 0
        for at in range(len(parts)):
            if at & bit:
                continue
            a, b = parts[at], parts[at | bit]
            parts[at] = jnp.where(low, a, pltpu.roll(b, shift, 1))
            parts[at | bit] = jnp.where(low, pltpu.roll(a, LANES - shift, 1), b)
        bit //= 2
    return parts


def pack_wire(plan, total_ref, wire_ref):
    px, group = plan.padded_x, plan.per_tile
    for half in range(plan.halves):
        for block in range(MODES // group):
            parts = [
                total_ref[pl.ds((block * group + j) * px, px), pl.ds(half * LANES, LANES)] for j in range(group)
            ]
            parts = swap_groups(parts, plan.width)
            owner_y, tile = block // plan.tiles, block % plan.tiles
            for g in range(group):
                target = (half * group + g) * plan.count_y + owner_y
                wire_ref[target, :, pl.ds(tile * LANES, LANES)] = parts[g].astype(BF16)


def unpack_wire(plan, wire_ref, spectrum_ref):
    px, group = plan.padded_x, plan.per_tile
    for half in range(plan.halves):
        for block in range(MODES // group):
            owner_y, tile = block // plan.tiles, block % plan.tiles
            parts = [
                wire_ref[(half * group + g) * plan.count_y + owner_y, :, pl.ds(tile * LANES, LANES)].astype(F32)
                for g in range(group)
            ]
            parts = swap_groups(parts, plan.width)
            for j in range(group):
                spectrum_ref[pl.ds((block * group + j) * px, px), pl.ds(half * LANES, LANES)] = parts[j].astype(BF16)


def analyse_block(plan, block, fields, third_ref, second_ref, total_ref, wire_ref):
    step = pl.program_id(0)
    inner = dot(fields, third_ref[0]) + dot(fields, third_ref[1])
    high, low = split(inner)
    part = dot(second_ref[0], high) + dot(second_ref[0], low) + dot(second_ref[1], high)

    @pl.when(step == 0)
    def _():
        total_ref[...] = part

    @pl.when(step > 0)
    def _():
        total_ref[...] += part

    @pl.when(step == plan.blocks - 1)
    def _():
        pack_wire(plan, total_ref, wire_ref)


def synthesise_block(plan, wire_ref, second_t_ref, third_t_ref, spectrum_ref, field_ref):
    @pl.when(pl.program_id(0) == 0)
    def _():
        unpack_wire(plan, wire_ref, spectrum_ref)

    spectrum = spectrum_ref[...]
    inner = (dot(second_t_ref[0], spectrum) + dot(second_t_ref[1], spectrum)).astype(BF16)
    field_ref[...] = dot(inner, third_t_ref[0]) + dot(inner, third_t_ref[1])


def gelu_slope(value):
    size = jnp.abs(value)
    t = 1.0 / (1.0 + (0.3275911 * 0.7071067811865476) * size)
    poly = 0.5 * 1.061405429
    for c in (-1.453152027, 1.421413741, -0.284496736, 0.254829592):
        poly = poly * t + 0.5 * c
    bell = jnp.exp(-0.5 * value * value)
    tail = bell * (poly * t - 0.3989422804014327 * size)
    return jnp.where(value >= 0, 1.0 - tail, tail)


CHUNK = 32


def each_chunk(plan, work):
    def step(k, carry):
        work(pl.ds(pl.multiple_of(k * CHUNK, CHUNK), CHUNK))
        return carry

    lax.fori_loop(0, plan.rows // CHUNK, step, 0)


def lanes_of(plan, channel):
    return pl.ds(channel * plan.length_z, plan.length_z)


def send_back(plan, rows, signals, mixing_ref, fields_ref, local_ref):
    for o, signal in enumerate(signals):
        fields_ref[rows, lanes_of(plan, o)] = signal.astype(BF16)
    for i in range(plan.channels):
        value = mixing_ref[0, i] * signals[0]
        for o in range(1, plan.channels):
            value = value + mixing_ref[o, i] * signals[o]
        local_ref[i, rows, :] = value.astype(BF16)


def input_kernel(plan, flags, act_ref, third_ref, second_ref, wire_ref, total_ref):
    fields = jnp.concatenate([act_ref[i] for i in range(plan.channels)], axis=1)
    analyse_block(plan, None, fields, third_ref, second_ref, total_ref, wire_ref)


def first_kernel(
    plan, flags, mixing_ref, bias_ref, act_ref, cot_ref, wire_in_ref, third_ref, third_t_ref, second_ref, second_t_ref,
    wire_ref, slope_ref, local_ref, total_ref, spectrum_ref, field_ref, fields_ref,
):
    synthesise_block(plan, wire_in_ref, second_t_ref, third_t_ref, spectrum_ref, field_ref)

    def work(rows):
        inputs = [act_ref[i, rows, :].astype(F32) for i in range(plan.channels)]
        signals = []
        for o in range(plan.channels):
            pre = field_ref[rows, lanes_of(plan, o)] + bias_ref[0, o]
            for i in range(plan.channels):
                pre = pre + mixing_ref[o, i] * inputs[i]
            slope = gelu_slope(pre)
            slope_ref[o, rows, :] = slope
            signals.append(cot_ref[o, rows, :].astype(F32) * slope)
        send_back(plan, rows, signals, mixing_ref, fields_ref, local_ref)

    each_chunk(plan, work)
    analyse_block(plan, None, fields_ref[...], third_ref, second_ref, total_ref, wire_ref)


def middle_kernel(
    plan, flags, mixing_ref, own_ref, other_ref, slope_ref, wire_in_ref, third_ref, third_t_ref, second_ref,
    second_t_ref, wire_ref, grad_ref, local_ref, total_ref, spectrum_ref, field_ref, fields_ref,
):
    synthesise_block(plan, wire_in_ref, second_t_ref, third_t_ref, spectrum_ref, field_ref)
    active = flags[1] > 0

    def work(rows):
        signals = []
        for i in range(plan.channels):
            local = jnp.where(active, own_ref[i, rows, :].astype(F32), other_ref[i, rows, :].astype(F32))
            grad = local + field_ref[rows, lanes_of(plan, i)]
            grad_ref[i, rows, :] = grad.astype(BF16)
            signals.append(grad * slope_ref[i, rows, :])
        send_back(plan, rows, signals, mixing_ref, fields_ref, local_ref)

    each_chunk(plan, work)
    analyse_block(plan, None, fields_ref[...], third_ref, second_ref, total_ref, wire_ref)


def last_kernel(
    plan, flags, own_ref, kept_ref, wire_in_ref, third_t_ref, second_t_ref, grad_ref, spectrum_ref, field_ref
):
    synthesise_block(plan, wire_in_ref, second_t_ref, third_t_ref, spectrum_ref, field_ref)
    active = flags[1] > 0

    def work(rows):
        for i in range(plan.channels):
            grad = own_ref[i, rows, :].astype(F32) + field_ref[rows, lanes_of(plan, i)]
            grad_ref[i, rows, :] = jnp.where(active, grad.astype(BF16), kept_ref[i, rows, :])

    each_chunk(plan, work)


def mode_sums(plan, wire_ref, first_ref):
    received = wire_ref[...].reshape(plan.devices * plan.padded_x, plan.own_second * plan.width)
    modes = dot(first_ref[0], received) + dot(first_ref[1], received)
    return modes.T.reshape(plan.pairs, plan.channels, MODES)


def mix_modes(plan, modes, weights_ref, backward):
    if not backward:
        mixed = weights_ref[:, 0] * modes[:, 0:1, :]
        for i in range(1, plan.channels):
            mixed = mixed + weights_ref[:, i] * modes[:, i : i + 1, :]
        return mixed
    row = lax.broadcasted_iota(jnp.int32, modes.shape, 1)
    mixed = jnp.zeros_like(modes)
    for i in range(plan.channels):
        mixed = jnp.where(row == i, jnp.sum(weights_ref[:, i] * modes, axis=1, keepdims=True), mixed)
    return mixed


def spread_modes(plan, mixed, first_t_ref, wire_out_ref):
    flat = mixed.reshape(plan.pairs * plan.channels, MODES)
    high, low = split(flat)

    def across(a, b):
        return lax.dot_general(a, b, (((1,), (1,)), ((), ())), preferred_element_type=F32)

    spread = across(first_t_ref[0], high) + across(first_t_ref[0], low) + across(first_t_ref[1], high)
    spread = spread.astype(BF16)
    for g in range(plan.count_x):
        piece = spread[g * plan.padded_x : (g + 1) * plan.padded_x]
        for h in range(plan.count_y):
            wire_out_ref[g * plan.count_y + h] = piece


def spectral_kernel(plan, backward, wire_ref, weights_ref, first_ref, first_t_ref, modes_ref, wire_out_ref):
    modes = mode_sums(plan, wire_ref, first_ref)
    modes_ref[...] = modes
    spread_modes(plan, mix_modes(plan, modes, weights_ref, backward), first_t_ref, wire_out_ref)


def mixing_kernel(plan, wire_ref, weights_ref, first_ref, modes_ref, mixed_ref):
    modes = mode_sums(plan, wire_ref, first_ref)
    modes_ref[...] = modes
    mixed_ref[...] = mix_modes(plan, modes, weights_ref, True)


def spread_kernel(plan, flags, own_ref, other_ref, first_t_ref, wire_out_ref):
    mixed = jnp.where(flags[1] > 0, own_ref[...], other_ref[...])
    spread_modes(plan, mixed, first_t_ref, wire_out_ref)


def params():
    return pltpu.CompilerParams(vmem_limit_bytes=VMEM_LIMIT)


class Calls:
    def __init__(self, plan):
        self.plan = p = plan
        self.field_block = pl.BlockSpec((p.channels, p.rows, p.length_z), lambda b, f: (0, b, 0))
        self.wire_block = pl.BlockSpec(p.wire, lambda b, f: (0, 0, 0))
        self.third = pl.BlockSpec(p.third.shape, lambda b, f: (0, 0, 0))
        self.third_t = pl.BlockSpec(p.third_t.shape, lambda b, f: (0, 0, 0))
        self.second = pl.BlockSpec((None, None) + p.second.shape[2:], lambda b, f: (f[0], b, 0, 0, 0))
        self.second_t = pl.BlockSpec((None, None) + p.second_t.shape[2:], lambda b, f: (f[0], b, 0, 0, 0))
        self.small = pl.BlockSpec(memory_space=pltpu.SMEM)
        self.total = pltpu.VMEM((MODES * p.padded_x, MODES * p.channels), F32)
        self.spectrum = pltpu.VMEM((MODES * p.padded_x, MODES * p.channels), BF16)
        self.field = pltpu.VMEM((p.rows, p.channels * p.length_z), F32)
        self.fields = pltpu.VMEM((p.rows, p.channels * p.length_z), BF16)
        self.wire_shape = jax.ShapeDtypeStruct(p.wire, BF16)
        self.modes_shape = jax.ShapeDtypeStruct((p.pairs, p.channels, MODES), F32)

    def field_shape(self, dtype):
        p = self.plan
        return jax.ShapeDtypeStruct((p.channels, p.rows_x * p.rows_y, p.length_z), dtype)

    def over_blocks(self, kernel, name, flags, args, in_specs, out_specs, out_shape, scratch):
        return pl.pallas_call(
            functools.partial(kernel, self.plan),
            grid_spec=pltpu.PrefetchScalarGridSpec(
                num_scalar_prefetch=1, grid=(self.plan.blocks,), in_specs=in_specs, out_specs=out_specs,
                scratch_shapes=scratch,
            ),
            out_shape=out_shape, compiler_params=params(), name=name,
        )(flags, *args)

    def whole(self, kernel, name, args, out_shape, flags=None):
        specs = [pl.BlockSpec(memory_space=pltpu.VMEM)] * len(args)
        if flags is not None:
            args, specs = (flags, *args), [self.small] + specs
        return pl.pallas_call(
            kernel, in_specs=specs,
            out_specs=jax.tree.map(lambda _: pl.BlockSpec(memory_space=pltpu.VMEM), out_shape),
            out_shape=out_shape, compiler_params=params(), name=name,
        )(*args)


def exchange(wire):
    return lax.all_to_all(wire, PLANE, split_axis=0, concat_axis=0, tiled=True)


def from_behind(block, distance):
    devices = range(lax.axis_size("segment"))
    route = [(i - distance, i) for i in devices if i - distance in devices]
    return lax.ppermute(block, "segment", route)


def body(activations, cotangent, spectral_weights, pointwise, channel_bias):
    _, channels, rows_x, rows_y, length_z = activations.shape
    plan = Plan(channels, rows_x, rows_y, length_z, lax.axis_size("gx"), lax.axis_size("gy"))
    calls = Calls(plan)
    act = activations.reshape(channels, rows_x * rows_y, length_z)
    cot = cotangent.reshape(channels, rows_x * rows_y, length_z)
    weights = spectral_weights.reshape(plan.pairs, channels, channels, MODES)
    mixing = pointwise[0]
    third, third_t = jnp.asarray(plan.third), jnp.asarray(plan.third_t)
    second, second_t = jnp.asarray(plan.second), jnp.asarray(plan.second_t)
    first, first_t = jnp.asarray(plan.first), jnp.asarray(plan.first_t)
    segment = lax.axis_index("segment")
    segments = lax.axis_size("segment")
    half = lax.axis_index("gy")

    def flags(turn):
        return jnp.stack([half, (segment == segments - 1 - turn).astype(jnp.int32)])

    wire = calls.over_blocks(
        input_kernel, "input_modes", flags(0), (act, third, second),
        [calls.field_block, calls.third, calls.second], calls.wire_block, calls.wire_shape, [calls.total],
    )
    input_modes, wire = calls.whole(
        functools.partial(spectral_kernel, plan, False), "mix_inputs", (exchange(wire), weights, first, first_t),
        (calls.modes_shape, calls.wire_shape),
    )
    wire, slope, local = calls.over_blocks(
        first_kernel, "first_signal", flags(0),
        (mixing, channel_bias, act, cot, exchange(wire), third, third_t, second, second_t),
        [calls.small, calls.small, calls.field_block, calls.field_block, calls.wire_block, calls.third, calls.third_t,
         calls.second, calls.second_t],
        [calls.wire_block, calls.field_block, calls.field_block],
        [calls.wire_shape, calls.field_shape(F32), calls.field_shape(BF16)],
        [calls.total, calls.spectrum, calls.field, calls.fields],
    )
    kept_grad = kept_modes = None
    for turn in range(segments - 1):
        active = segment == segments - 1 - turn
        other_local = from_behind(local, -1)
        modes, mixed = calls.whole(
            functools.partial(mixing_kernel, plan), "mix_signal", (exchange(wire), weights, first),
            (calls.modes_shape, calls.modes_shape),
        )
        kept_modes = modes if kept_modes is None else jnp.where(active, modes, kept_modes)
        wire = calls.whole(
            functools.partial(spread_kernel, plan), "spread_signal", (mixed, from_behind(mixed, -1), first_t),
            calls.wire_shape, flags(turn),
        )
        wire, grad, local = calls.over_blocks(
            middle_kernel, "next_signal", flags(turn),
            (mixing, local, other_local, slope, exchange(wire), third, third_t, second, second_t),
            [calls.small, calls.field_block, calls.field_block, calls.field_block, calls.wire_block, calls.third,
             calls.third_t, calls.second, calls.second_t],
            [calls.wire_block, calls.field_block, calls.field_block],
            [calls.wire_shape, calls.field_shape(BF16), calls.field_shape(BF16)],
            [calls.total, calls.spectrum, calls.field, calls.fields],
        )
        kept_grad = grad if kept_grad is None else jnp.where(active, grad, kept_grad)
    modes, wire = calls.whole(
        functools.partial(spectral_kernel, plan, True), "mix_last", (exchange(wire), weights, first, first_t),
        (calls.modes_shape, calls.wire_shape),
    )
    if kept_modes is not None:
        modes = jnp.where(segment == 0, modes, kept_modes)
    weight_grad = input_modes[:, :, None, :] * modes[:, None, :, :]
    grad = calls.over_blocks(
        last_kernel, "last_grad", flags(segments - 1),
        (local, local if kept_grad is None else kept_grad, exchange(wire), third_t, second_t),
        [calls.field_block, calls.field_block, calls.wire_block, calls.third_t, calls.second_t],
        calls.field_block, calls.field_shape(BF16), [calls.spectrum, calls.field],
    )
    return (
        grad.reshape(activations.shape),
        weight_grad.reshape(spectral_weights.shape),
    )


def solution(mesh):
    return jax.shard_map(
        body,
        mesh=mesh,
        in_specs=(
            P("segment", "groups", "gx", "gy", None),
            P("groups", "gx", "gy", None),
            P("segment", "gy", "gx", None, None, None),
            P("segment", None, None),
            P("segment", None),
        ),
        out_specs=(
            P("segment", "groups", "gx", "gy", None),
            P("segment", "gy", "gx", "groups", None, None),
        ),
        check_vma=False,
    )
```

```python
import functools
import math

import jax
import jax.numpy as jnp
import ml_dtypes
import numpy as np
from jax import lax
from jax.experimental import pallas as pl
from jax.experimental.pallas import tpu as pltpu
from jax.sharding import PartitionSpec as P

MODES = 32
LANES = 128
PLANE = ("gx", "gy")
WHOLE = ("segment",) + PLANE
F32 = jnp.float32
BF16 = jnp.bfloat16
VMEM_LIMIT = 28 * 1024 * 1024


def trig_basis(length):
    half = MODES // 2
    points = np.arange(length)[None, :]
    freqs = np.arange(half)[:, None]
    angle = 2.0 * math.pi / length
    rows = np.concatenate(
        [np.cos((freqs * points % length) * angle), np.sin(((freqs + 1) * points % length) * angle)], axis=0
    )
    scales = np.where(np.arange(MODES) == 0, 1.0 / math.sqrt(length), math.sqrt(2.0 / length))
    return rows * scales[:, None]


def high_low(values):
    high = values.astype(np.float32).astype(ml_dtypes.bfloat16)
    low = (values - high.astype(np.float64)).astype(np.float32).astype(ml_dtypes.bfloat16)
    return np.stack([high, low])


class Plan:
    def __init__(self, channels, rows_x, rows_y, length_z, count_x, count_y):
        self.channels, self.length_z = channels, length_z
        self.count_x, self.count_y = count_x, count_y
        self.devices = count_x * count_y
        share = rows_x // count_y
        self.side = share * rows_y
        self.rows = self.side * count_y
        self.block = min(128, self.side // 2)
        self.steps = self.side // self.block // 2
        self.pieces = self.steps * count_y
        self.piece = self.rows // self.pieces
        self.own_third = MODES // count_x
        self.own_second = MODES // count_y
        self.width = self.own_third * channels
        self.parts = 2 if share <= 8 and self.own_second // 2 * self.width >= LANES else 1
        padded = 8 if self.parts == 2 else -(-share // 16) * 16
        self.in_part = self.own_second // self.parts
        self.slot = self.parts * padded
        self.per_tile = LANES // self.width
        self.tiles = self.in_part // self.per_tile
        self.groups = MODES // self.parts // self.per_tile
        self.halves = MODES * channels // LANES
        self.lanes = self.in_part * self.width
        self.wire = (self.devices, self.slot, self.lanes)
        self.modes = self.own_second * self.own_third
        self.spectrum = (MODES * padded, MODES * channels)
        self.field = (channels, self.rows, length_z)
        along_x = trig_basis(rows_x * count_x).reshape(MODES, self.devices, share)
        along_y = trig_basis(rows_y * count_y).reshape(MODES, count_y, rows_y)
        along_z = trig_basis(length_z)
        third = np.einsum("ik,cz->izck", np.eye(channels), along_z)
        third = third.reshape(channels * length_z, MODES * channels)
        self.third = high_low(third)
        self.third_t = high_low(third.T)
        order = [[(own + k) % count_y for k in range(count_y)] for own in range(count_y)]
        slabs = along_y[:, np.array(order)].reshape(count_y, self.parts, self.in_part, count_y, count_y, rows_y)
        second = np.einsum("opqdsy,xk->doqpxsky", slabs, np.eye(padded, share))
        second = second.reshape(count_y, MODES * padded, self.rows)
        self.second = np.moveaxis(high_low(second), 0, 1)
        self.second_t = np.moveaxis(high_low(np.swapaxes(second, 1, 2)), 0, 1)
        spread = np.zeros((MODES, self.devices, padded))
        spread[:, :, :share] = along_x
        first = np.einsum("pq,adx->padqx", np.eye(self.parts), spread)
        first = first.reshape(self.parts * MODES, self.devices * self.slot)
        self.first = high_low(first)
        self.first_t = high_low(first.T)


def dot(a, b):
    return jnp.dot(a, b, preferred_element_type=F32)


def join(arrays, axis):
    return jnp.concatenate(arrays, axis=axis)


def split(value):
    high = value.astype(BF16)
    return high, (value - high.astype(F32)).astype(BF16)


def swap_groups(parts, width):
    parts = list(parts)
    lane = lax.broadcasted_iota(jnp.int32, parts[0].shape, 1)
    bit = len(parts) // 2
    while bit:
        shift = bit * width
        low = (lane // shift) % 2 == 0
        for at in range(len(parts)):
            if at & bit:
                continue
            a, b = parts[at], parts[at | bit]
            parts[at] = jnp.where(low, a, pltpu.roll(b, shift, 1))
            parts[at | bit] = jnp.where(low, pltpu.roll(a, LANES - shift, 1), b)
        bit //= 2
    return parts


def pack_wire(plan, total_ref, wire_ref):
    slot, group = plan.slot, plan.per_tile
    for half in range(plan.halves):
        for block in range(plan.groups):
            parts = [
                total_ref[pl.ds((block * group + j) * slot, slot), pl.ds(half * LANES, LANES)] for j in range(group)
            ]
            parts = swap_groups(parts, plan.width)
            owner_y, tile = block // plan.tiles, block % plan.tiles
            for g in range(group):
                target = (half * group + g) * plan.count_y + owner_y
                wire_ref[target, :, pl.ds(tile * LANES, LANES)] = parts[g].astype(BF16)


def unpack_wire(plan, load, spectrum_ref):
    slot, group = plan.slot, plan.per_tile
    for half in range(plan.halves):
        for block in range(plan.groups):
            owner_y, tile = block // plan.tiles, block % plan.tiles
            parts = [
                load((half * group + g) * plan.count_y + owner_y, pl.ds(tile * LANES, LANES)).astype(F32)
                for g in range(group)
            ]
            parts = swap_groups(parts, plan.width)
            for j in range(group):
                spectrum_ref[pl.ds((block * group + j) * slot, slot), pl.ds(half * LANES, LANES)] = parts[j].astype(BF16)


def blocks_of(wire_ref):
    return lambda device, lanes: wire_ref[device, :, lanes]


def synthesise(plan, load, second_t, spectrum_ref, inner_ref):
    unpack_wire(plan, load, spectrum_ref)
    spectrum = spectrum_ref[...]
    inner_ref[...] = dot(join([second_t(0), second_t(1)], 1), join([spectrum, spectrum], 0)).astype(BF16)


def piece_rows(plan, k):
    return pl.ds(pl.multiple_of(k * plan.piece, 16), plan.piece)


def run_blocks(plan, inner_ref, third_t_ref, slots, work, third_ref=None, sums_ref=None, leaving=()):
    fields, signals = slots[:2], slots[2:]
    per_side = plan.side // plan.block
    count = per_side * plan.count_y

    def rows_of(k):
        return pl.ds(pl.multiple_of(k * plan.block, 16), plan.block)

    def cells(k, ref):
        inner = inner_ref[rows_of(k), :]
        ref[...] = dot(join([inner, inner], 1), join([third_t_ref[0], third_t_ref[1]], 0))

    def sums(k, ref):
        if third_ref is not None:
            values = ref[...]
            sums_ref[rows_of(k), :] = dot(join([values, values], 1), join([third_ref[0], third_ref[1]], 0))

    cells(0, fields[0])
    if third_ref is not None:
        signals[1][...] = jnp.zeros_like(signals[1])
    for y in range(plan.count_y):

        def one(step, carry):
            here = 2 * step
            k = y * per_side + here
            sums(lax.rem(k + count - 1, count), signals[1])
            cells(k + 1, fields[1])
            work(y, rows_of(here), rows_of(k), fields[0], signals[0])
            sums(k, signals[0])
            cells(lax.rem(k + 2, count), fields[0])
            work(y, rows_of(here + 1), rows_of(k + 1), fields[1], signals[1])
            piece = y * plan.steps + step
            for ref, target, sems in leaving:
                rows = piece_rows(plan, piece)
                pltpu.make_async_copy(ref.at[:, rows], target.at[:, rows], sems.at[piece]).start()
            return carry

        lax.fori_loop(0, plan.steps, one, 0)
    sums(count - 1, signals[1])


def wait_pieces(plan, leaving):
    for ref, target, sems in leaving:
        for p in range(plan.pieces):
            rows = piece_rows(plan, p)
            pltpu.make_async_copy(ref.at[:, rows], target.at[:, rows], sems.at[p]).wait()


def finish(plan, sums_ref, second, total_ref, wire_ref):
    high, low = split(sums_ref[...])
    total_ref[...] = dot(join([second(0), second(0), second(1)], 1), join([high, low, high], 0))
    pack_wire(plan, total_ref, wire_ref)


def gelu_slope(value):
    size = jnp.abs(value)
    t = 1.0 / (1.0 + (0.3275911 * 0.7071067811865476) * size)
    poly = 0.5 * 1.061405429
    for c in (-1.453152027, 1.421413741, -0.284496736, 0.254829592):
        poly = poly * t + 0.5 * c
    bell = jnp.exp(-0.5 * value * value)
    tail = bell * (poly * t - 0.3989422804014327 * size)
    return jnp.where(value >= 0, 1.0 - tail, tail)


def each_chunk(total, chunk, work):
    def step(k, carry):
        work(pl.ds(pl.multiple_of(k * chunk, chunk), chunk))
        return carry

    lax.fori_loop(0, total // chunk, step, 0)


def shifted(rows, by):
    return pl.ds(pl.multiple_of(rows.start + by, 16), rows.size)


def lanes_of(plan, channel):
    return pl.ds(channel * plan.length_z, plan.length_z)


def mixed_with(plan, mixing_ref, values, out, transposed):
    total = None
    for k, value in enumerate(values):
        term = (mixing_ref[k, out] if transposed else mixing_ref[out, k]) * value
        total = term if total is None else total + term
    return total


def starts(copies, sems):
    copies = [pltpu.make_async_copy(source, target, sems.at[k]) for k, (source, target) in enumerate(copies)]
    for copy in copies:
        copy.start()
    return copies


def waits(copies):
    for copy in copies:
        copy.wait()


def side(plan, k):
    return pl.ds(k * plan.side, plan.side)


def own_side(plan, flags, k=0):
    at = flags[0] if k == 0 else 1 - flags[0]
    return pl.ds(pl.multiple_of(at * plan.side, 16), plan.side)


def input_kernel(
    plan, flags, act_hbm, third_hbm, second_hbm, other_ref, wire_ref, own_ref, third_ref, second_ref, sums_ref,
    total_ref, sems,
):
    copies = starts(
        [(third_hbm, third_ref), (act_hbm.at[:, own_side(plan, flags)], own_ref),
         (second_hbm.at[flags[0]], second_ref)], sems,
    )
    waits(copies[:2])
    fields = join([join([ref[i] for i in range(plan.channels)], 1) for ref in (own_ref, other_ref)], 0)
    sums_ref[...] = dot(join([fields, fields], 1), join([third_ref[0], third_ref[1]], 0))
    waits(copies[2:])
    finish(plan, sums_ref, lambda k: second_ref[k], total_ref, wire_ref)


CHUNK = 32


def chunks_of(plan, *spans):
    for at in range(0, plan.block, CHUNK):
        yield *(pl.ds(pl.multiple_of(rows.start + at, 16), CHUNK) for rows in spans), pl.ds(at, CHUNK)


def cells_of(plan, flags, own_ref, other_ref):
    def load(y, channel, rows):
        if y == 0:
            rows = pl.ds(pl.multiple_of(flags[0] * plan.side + rows.start, 16), rows.size)
        return (other_ref if y else own_ref)[channel, rows, :].astype(F32)

    return load


def slopes(plan, mixing_ref, load_input, y, there, here, cells_ref):
    inputs = [load_input(y, i, there) for i in range(plan.channels)]
    for o in range(plan.channels):
        pre = mixed_with(plan, mixing_ref, inputs, o, False) + mixing_ref[o, plan.channels]
        yield gelu_slope(pre + cells_ref[here, lanes_of(plan, o)])


def first_kernel(
    plan, segments, flags, mixing_ref, act_ref, cot_ref, act_other_ref, cot_other_ref, wire_in_ref, third_ref,
    third_t_ref, second_ref, second_t_ref, wire_ref, kept_hbm,
    kept_ref, total_ref, spectrum_ref, inner_ref, sums_ref, field_a, field_b, signal_a, signal_b, sems,
):
    half, last = flags[0], flags[1] == segments - 1
    load_input = cells_of(plan, flags, act_ref, act_other_ref)
    load_cotangent = cells_of(plan, flags, cot_ref, cot_other_ref)
    synthesise(plan, blocks_of(wire_in_ref), lambda k: second_t_ref[half, k], spectrum_ref, inner_ref)
    slots = [field_a, field_b, signal_a, signal_b]
    leaving = [(kept_ref, kept_hbm, sems)]

    @pl.when(last)
    def _():
        def work(y, in_side, rows, cells, out):
            for there, everywhere, here in chunks_of(plan, in_side, rows):
                for o, slope in enumerate(slopes(plan, mixing_ref, load_input, y, there, here, cells)):
                    signal = load_cotangent(y, o, there) * slope
                    kept_ref[o, everywhere, :] = signal
                    out[here, lanes_of(plan, o)] = signal.astype(BF16)

        run_blocks(plan, inner_ref, third_t_ref, slots, work, third_ref, sums_ref, leaving)
        finish(plan, sums_ref, lambda k: second_ref[half, k], total_ref, wire_ref)

    @pl.when(jnp.logical_not(last))
    def _():
        def work(y, in_side, rows, cells, out):
            for there, everywhere, here in chunks_of(plan, in_side, rows):
                for o, slope in enumerate(slopes(plan, mixing_ref, load_input, y, there, here, cells)):
                    kept_ref[o, everywhere, :] = slope

        run_blocks(plan, inner_ref, third_t_ref, slots, work, leaving=leaving)

    wait_pieces(plan, leaving)


def shared_kernel(
    plan, flags, mixing_ref, act_own_ref, act_other_ref, cot_ref, cot_other_ref, wire_ref, third_t_ref, second_t_ref,
    local_hbm, local_ref, spectrum_ref, inner_ref, field_a, field_b, sems,
):
    half = flags[0]
    load_cotangent = cells_of(plan, flags, cot_ref, cot_other_ref)
    synthesise(plan, blocks_of(wire_ref), lambda k: second_t_ref[half, k], spectrum_ref, inner_ref)

    def load_input(y, channel, rows):
        return (act_other_ref if y else act_own_ref)[channel, rows, :].astype(F32)

    def work(y, in_side, rows, cells, out):
        for there, everywhere, here in chunks_of(plan, in_side, rows):
            signals = [
                load_cotangent(y, o, there) * slope
                for o, slope in enumerate(slopes(plan, mixing_ref, load_input, y, there, here, cells))
            ]
            for i in range(plan.channels):
                local_ref[i, everywhere, :] = mixed_with(plan, mixing_ref, signals, i, True)

    leaving = [(local_ref, local_hbm, sems)]
    run_blocks(plan, inner_ref, third_t_ref, [field_a, field_b, None, None], work, leaving=leaving)
    wait_pieces(plan, leaving)


def middle_kernel(
    plan, segments, turn, flags, mixing_ref, local_ref, kept_ref, wire_in_ref, third_ref, third_t_ref, second_ref,
    second_t_ref, wire_ref, local_out_hbm,
    local_out_ref, total_ref, spectrum_ref, inner_ref, sums_ref, field_a, field_b, signal_a, signal_b, sems,
):
    half, segment = flags[0], flags[1]
    active = segments - 1 - turn
    leaving = [(local_out_ref, local_out_hbm, sems)]

    @pl.when(segment < active)
    def _():
        synthesise(plan, lambda device, lanes: wire_in_ref[active * plan.devices + device, :, lanes],
                   lambda k: second_t_ref[half, k], spectrum_ref, inner_ref)

        def work(y, in_side, rows, cells, out):
            for there, here in chunks_of(plan, rows):
                signals = []
                for i in range(plan.channels):
                    grad = local_ref[i, there, :] + cells[here, lanes_of(plan, i)]
                    signals.append(grad * kept_ref[i, there, :])
                    out[here, lanes_of(plan, i)] = signals[i].astype(BF16)
                for i in range(plan.channels):
                    local_out_ref[i, there, :] = mixed_with(plan, mixing_ref, signals, i, True)

        run_blocks(plan, inner_ref, third_t_ref, [field_a, field_b, signal_a, signal_b], work, third_ref, sums_ref,
                   leaving)
        finish(plan, sums_ref, lambda k: second_ref[half, k], total_ref, wire_ref)
        wait_pieces(plan, leaving)

    @pl.when(segment >= active)
    def _():
        if turn == 0:
            def work(rows):
                signals = [kept_ref[o, rows, :] for o in range(plan.channels)]
                for i in range(plan.channels):
                    local_out_ref[i, rows, :] = mixed_with(plan, mixing_ref, signals, i, True)

            each_chunk(plan.rows, 32, work)
            waits(starts([(local_out_ref, local_out_hbm)], sems))
        else:
            waits(starts([(local_ref, local_out_hbm)], sems))


def side_grads(plan, segments, y, flags, local_ref, third_t_ref, second_t_ref, wire_in_ref, kept_wire_ref, grad_ref,
               spectrum_ref, inner_ref, field_ref):
    half, segment = flags[0], flags[1]
    last = (segments - 1) * plan.devices

    def load(device, lanes):
        return jnp.where(segment == 0, wire_in_ref[device, :, lanes], kept_wire_ref[last + device, :, lanes])

    synthesise(plan, load, lambda p: second_t_ref[half, p, side(plan, y), :], spectrum_ref, inner_ref)
    inner = inner_ref[...]
    field_ref[...] = dot(join([inner, inner], 1), join([third_t_ref[0], third_t_ref[1]], 0))

    def work(rows):
        there = shifted(rows, y * plan.side)
        for i in range(plan.channels):
            grad_ref[i, rows, :] = (local_ref[i, there, :] + field_ref[rows, lanes_of(plan, i)]).astype(BF16)

    each_chunk(plan.side, 64, work)


def last_other_kernel(
    plan, segments, flags, local_ref, third_t_ref, second_t_ref, wire_in_ref, kept_wire_ref, input_modes_ref,
    modes_ref, kept_modes_ref, grad_ref, weight_hbm, spectrum_ref, inner_ref, field_ref, sems, weight_ref,
):
    modes = jnp.where(flags[1] == 0, modes_ref[...], kept_modes_ref[...])
    for i in range(plan.channels):
        weight_ref[:, i] = input_modes_ref[:, i : i + 1, :] * modes
    copies = starts([(weight_ref, weight_hbm)], sems)
    side_grads(plan, segments, 1, flags, local_ref, third_t_ref, second_t_ref, wire_in_ref, kept_wire_ref, grad_ref,
               spectrum_ref, inner_ref, field_ref)
    waits(copies)


def last_own_kernel(
    plan, segments, flags, local_ref, third_t_ref, second_t_ref, wire_in_ref, kept_wire_ref, out_hbm,
    spectrum_ref, inner_ref, field_ref, sems, grad_ref,
):
    side_grads(plan, segments, 0, flags, local_ref, third_t_ref, second_t_ref, wire_in_ref, kept_wire_ref, grad_ref,
               spectrum_ref, inner_ref, field_ref)
    waits(starts([(grad_ref, out_hbm.at[:, own_side(plan, flags)])], sems))


def place_kernel(plan, flags, part_hbm, received_ref, out_hbm, sems):
    waits(starts([(received_ref, out_hbm.at[:, own_side(plan, flags, 1)])], sems))


def nothing_kernel(unused, out_hbm):
    pass


def mode_sums(plan, wire_ref, first_ref):
    received = wire_ref[...].reshape(plan.devices * plan.slot, plan.lanes)
    sums = dot(first_ref[0], received) + dot(first_ref[1], received)
    modes = join([sums[p * MODES : (p + 1) * MODES].T for p in range(plan.parts)], 0)
    return modes.reshape(plan.modes, plan.channels, MODES)


def flatten(plan, mixed):
    rows = mixed.reshape(plan.parts, plan.lanes, MODES)
    return join([rows[p].T for p in range(plan.parts)], 0).astype(BF16)


def mix_modes(plan, modes, weights_ref, backward):
    if not backward:
        mixed = weights_ref[:, 0] * modes[:, 0:1, :]
        for i in range(1, plan.channels):
            mixed = mixed + weights_ref[:, i] * modes[:, i : i + 1, :]
        return mixed
    row = lax.broadcasted_iota(jnp.int32, modes.shape, 1)
    mixed = jnp.zeros_like(modes)
    for i in range(plan.channels):
        mixed = jnp.where(row == i, jnp.sum(weights_ref[:, i] * modes, axis=1, keepdims=True), mixed)
    return mixed


def spread_modes(plan, mixed, first_t_ref):
    flat = flatten(plan, mixed)
    return (dot(first_t_ref[0], flat) + dot(first_t_ref[1], flat)).astype(BF16).reshape(plan.wire)


def spectral_kernel(plan, backward, wire_ref, weights_ref, first_ref, first_t_ref, modes_ref, wire_out_ref):
    modes = mode_sums(plan, wire_ref, first_ref)
    modes_ref[...] = modes
    spread = spread_modes(plan, mix_modes(plan, modes, weights_ref, backward), first_t_ref)
    copies = wire_out_ref.shape[0] // plan.devices
    for k in range(copies):
        wire_out_ref[pl.ds(k * plan.devices, plan.devices)] = spread


VMEM = pl.BlockSpec(memory_space=pltpu.VMEM)
SMEM = pl.BlockSpec(memory_space=pltpu.SMEM)
HBM = pl.BlockSpec(memory_space=pltpu.HBM)


def call(kernel, name, args, out_shape, scratch=(), scalars=0, far=0, aliases={}):
    specs = [SMEM] * scalars + [HBM] * far + [VMEM] * (len(args) - scalars - far)
    args = [
        pltpu.with_memory_space_constraint(arg, pltpu.HBM) if spec is HBM else arg for arg, spec in zip(args, specs)
    ]
    outs = out_shape if isinstance(out_shape, tuple) else (out_shape,)
    out_specs = tuple(VMEM if isinstance(out, jax.ShapeDtypeStruct) else HBM for out in outs)
    result = pl.pallas_call(
        kernel, in_specs=specs, out_specs=out_specs, out_shape=outs, scratch_shapes=scratch,
        input_output_aliases=aliases,
        compiler_params=pltpu.CompilerParams(vmem_limit_bytes=VMEM_LIMIT), name=name,
    )(*args)
    return result if isinstance(out_shape, tuple) else result[0]


def exchange(wire, axes=PLANE):
    return lax.all_to_all(wire, axes, split_axis=0, concat_axis=0, tiled=True)


def from_behind(block, distance):
    devices = range(lax.axis_size("segment"))
    route = [(i - distance, i) for i in devices if i - distance in devices]
    return lax.ppermute(block, "segment", route)


def other_core(block):
    return lax.ppermute(block, "gy", [(0, 1), (1, 0)])


def body(activations, cotangent, spectral_weights, pointwise, channel_bias):
    _, channels, rows_x, rows_y, length_z = activations.shape
    plan = Plan(channels, rows_x, rows_y, length_z, lax.axis_size("gx"), lax.axis_size("gy"))
    act = activations.reshape(plan.field)
    cot = cotangent.reshape(plan.field)
    weights = spectral_weights.reshape(plan.modes, channels, channels, MODES)
    mixing = jnp.concatenate([pointwise[0], channel_bias[0][:, None]], axis=1)
    third, third_t = jnp.asarray(plan.third), jnp.asarray(plan.third_t)
    second, second_t = jnp.asarray(plan.second), jnp.asarray(plan.second_t)
    first, first_t = jnp.asarray(plan.first), jnp.asarray(plan.first_t)
    segment = lax.axis_index("segment")
    segments = lax.axis_size("segment")
    half = lax.axis_index("gy")

    wire_shape = jax.ShapeDtypeStruct(plan.wire, BF16)
    wires_shape = jax.ShapeDtypeStruct((segments * plan.devices,) + plan.wire[1:], BF16)
    modes_shape = jax.ShapeDtypeStruct((plan.modes, channels, MODES), F32)
    part_shape = (channels, plan.side, length_z)
    wide = pltpu.HBM(plan.field, F32)
    wide_scratch = pltpu.VMEM(plan.field, F32)
    sums = pltpu.VMEM((plan.rows, MODES * channels), F32)
    inner = pltpu.VMEM((plan.rows, MODES * channels), BF16)
    total = pltpu.VMEM(plan.spectrum, F32)
    spectrum = pltpu.VMEM(plan.spectrum, BF16)
    field = pltpu.VMEM((plan.block, channels * length_z), F32)
    signal = pltpu.VMEM((plan.block, channels * length_z), BF16)
    flags = jnp.stack([half, segment])

    def sems(count):
        return pltpu.SemaphoreType.DMA((count,))

    both_ways = [total, spectrum, inner, sums, field, field, signal, signal, sems(plan.pieces)]

    def part_of(block, at):
        return lax.dynamic_slice_in_dim(block, at * plan.side, plan.side, 1)

    act_other = other_core(part_of(act, 1 - half))
    if segments > 1:
        next_own, mixing_next = from_behind(part_of(act, half), -1), from_behind(mixing, -1)
        next_other = from_behind(act_other, -1)
    wire = call(
        functools.partial(input_kernel, plan), "input_modes", (flags, act, third, second, act_other), wire_shape,
        [pltpu.VMEM(part_shape, BF16), pltpu.VMEM(plan.third.shape, BF16), pltpu.VMEM(plan.second.shape[1:], BF16),
         sums, total, sems(3)], 1, 3,
    )
    cot_later, wire = lax.optimization_barrier((cot, wire))
    cot_other = other_core(part_of(cot_later, 1 - half))
    input_modes, wire = call(
        functools.partial(spectral_kernel, plan, False), "mix_inputs", (exchange(wire), weights, first, first_t),
        (modes_shape, wire_shape),
    )
    wire_in = exchange(wire)
    wire, kept = call(
        functools.partial(first_kernel, plan, segments), "first_signal",
        (flags, mixing, act, cot, act_other, cot_other, wire_in, third, third_t, second, second_t),
        (wire_shape, wide), [wide_scratch] + both_ways, 2,
    )

    def mix_signal(wire, count):
        return call(
            functools.partial(spectral_kernel, plan, True), "mix_signal", (exchange(wire), weights, first, first_t),
            (modes_shape, jax.ShapeDtypeStruct((count * plan.devices,) + plan.wire[1:], BF16)),
        )

    def of_last():
        local = call(nothing_kernel, "no_local", (flags,), wide, scalars=1)
        return *mix_signal(wire, segments), local

    def of_others():
        local = call(
            functools.partial(shared_kernel, plan), "shared",
            (flags, mixing_next, next_own, next_other, cot, cot_other, wire_next, third_t, second_t), wide,
            [wide_scratch, spectrum, inner, field, field, sems(plan.pieces)], 2,
        )
        no_wires = call(nothing_kernel, "no_wires", (flags,), wires_shape, scalars=1)
        return input_modes, no_wires, local

    kept_wire = kept_modes = None
    local = kept
    for turn in range(segments - 1):
        active = segment == segments - 1 - turn
        if turn == 0:
            wire_next = from_behind(wire_in, -1)
            modes, wire, local = lax.cond(active, of_last, of_others)
        else:
            ahead = from_behind(local.astype(BF16), -1).astype(F32)
            local = jnp.where(segment == segments - 2 - turn, ahead, local)
            modes, wire = mix_signal(wire, segments)
        kept_modes = modes if kept_modes is None else jnp.where(active, modes, kept_modes)
        wires = exchange(wire, WHOLE)
        if kept_wire is None:
            kept_wire = wires
        else:
            here = lax.slice_in_dim(wires, (segments - 1 - turn) * plan.devices, (segments - turn) * plan.devices)
            old = lax.slice_in_dim(kept_wire, (segments - 1) * plan.devices, segments * plan.devices)
            kept_wire = jnp.concatenate(
                [kept_wire[: (segments - 1) * plan.devices], jnp.where(active, here, old)], axis=0
            )
        wire, local = call(
            functools.partial(middle_kernel, plan, segments, turn), "next_signal",
            (flags, mixing, local, kept, wires, third, third_t, second, second_t), (wire_shape, wide),
            [wide_scratch] + both_ways, 2,
        )
    if segments == 1:
        local = jnp.einsum("oi,oyz->iyz", pointwise[0], kept, precision=lax.Precision.HIGHEST)
    modes, wire = mix_signal(wire, 1)
    wire = exchange(wire)
    args = (flags, local, third_t, second_t, wire, wire if kept_wire is None else kept_wire)
    scratch = [spectrum, pltpu.VMEM((plan.side, MODES * channels), BF16),
               pltpu.VMEM((plan.side, channels * length_z), F32), sems(1)]
    weight_shape = (plan.modes, channels, channels, MODES)
    other_grads, weight_grad = call(
        functools.partial(last_other_kernel, plan, segments), "last_other",
        args + (input_modes, modes, modes if kept_modes is None else kept_modes),
        (jax.ShapeDtypeStruct(part_shape, BF16), pltpu.HBM(weight_shape, F32)),
        scratch + [pltpu.VMEM(weight_shape, F32)], 1,
    )
    received = other_core(other_grads)
    grad = call(
        functools.partial(last_own_kernel, plan, segments), "last_own", args, pltpu.HBM(plan.field, BF16),
        scratch + [pltpu.VMEM(part_shape, BF16)], 1,
    )
    grad = call(
        functools.partial(place_kernel, plan), "place", (flags, grad, received), pltpu.HBM(plan.field, BF16),
        [sems(1)], 1, 1, {1: 0},
    )
    return grad.reshape(activations.shape), weight_grad.reshape(spectral_weights.shape)


def solution(mesh):
    return jax.shard_map(
        body,
        mesh=mesh,
        in_specs=(
            P("segment", "groups", "gx", "gy", None),
            P("groups", "gx", "gy", None),
            P("segment", "gy", "gx", None, None, None),
            P("segment", None, None),
            P("segment", None),
        ),
        out_specs=(
            P("segment", "groups", "gx", "gy", None),
            P("segment", "gy", "gx", "groups", None, None),
        ),
        check_vma=False,
    )
```

```python
import functools
import math

import jax
import jax.numpy as jnp
import ml_dtypes
import numpy as np
from jax import lax
from jax.experimental import pallas as pl
from jax.experimental.pallas import tpu as pltpu
from jax.sharding import PartitionSpec as P

MODES = 32
LANES = 128
PLANE = ("gx", "gy")
WHOLE = ("segment",) + PLANE
F32 = jnp.float32
BF16 = jnp.bfloat16
VMEM_LIMIT = 22 * 1024 * 1024
CHUNK = 64


def trig_basis(length):
    half = MODES // 2
    points = np.arange(length)[None, :]
    freqs = np.arange(half)[:, None]
    angle = 2.0 * math.pi / length
    rows = np.concatenate(
        [np.cos((freqs * points % length) * angle), np.sin(((freqs + 1) * points % length) * angle)], axis=0
    )
    scales = np.where(np.arange(MODES) == 0, 1.0 / math.sqrt(length), math.sqrt(2.0 / length))
    return rows * scales[:, None]


def high_low(values):
    high = values.astype(np.float32).astype(ml_dtypes.bfloat16)
    low = (values - high.astype(np.float64)).astype(np.float32).astype(ml_dtypes.bfloat16)
    return np.stack([high, low])


class Plan:
    def __init__(self, channels, rows_x, rows_y, length_z, count_x, count_y):
        self.channels, self.length_z = channels, length_z
        self.count_x, self.count_y = count_x, count_y
        self.devices = count_x * count_y
        share = rows_x // count_y
        self.side = share * rows_y
        self.rows = self.side * count_y
        self.pieces = 2 * count_y
        self.piece = self.rows // self.pieces
        self.own_third = MODES // count_x
        self.own_second = MODES // count_y
        self.width = self.own_third * channels
        self.parts = 2 if share <= 8 and self.own_second // 2 * self.width >= LANES else 1
        padded = 8 if self.parts == 2 else -(-share // 16) * 16
        self.in_part = self.own_second // self.parts
        self.slot = self.parts * padded
        self.per_tile = LANES // self.width
        self.tiles = self.in_part // self.per_tile
        self.groups = MODES // self.parts // self.per_tile
        self.halves = MODES * channels // LANES
        self.lanes = self.in_part * self.width
        self.wire = (self.devices, self.slot, self.lanes)
        self.modes = self.own_second * self.own_third
        self.spectrum = (MODES * padded, MODES * channels)
        self.field = (channels, self.rows, length_z)
        along_x = trig_basis(rows_x * count_x).reshape(MODES, self.devices, share)
        along_y = trig_basis(rows_y * count_y).reshape(MODES, count_y, rows_y)
        along_z = trig_basis(length_z)
        third = np.einsum("ik,cz->izck", np.eye(channels), along_z)
        third = third.reshape(channels * length_z, MODES * channels)
        self.third = high_low(third)
        self.third_t = high_low(third.T)[0]
        slabs = along_y.reshape(count_y, self.parts, self.in_part, count_y, rows_y)
        second = np.einsum("opqsy,xk->oqpxsky", slabs, np.eye(padded, share))
        second = second.reshape(MODES * padded, self.rows)
        self.second = high_low(second)
        self.second_t = high_low(second.T)[0]
        spread = np.zeros((MODES, self.devices, padded))
        spread[:, :, :share] = along_x
        first = np.einsum("pq,adx->padqx", np.eye(self.parts), spread)
        first = first.reshape(self.parts * MODES, self.devices * self.slot)
        self.first = high_low(first)
        self.first_t = high_low(first.T)


def dot(a, b):
    return jnp.dot(a, b, preferred_element_type=F32)


def join(arrays, axis):
    return jnp.concatenate(arrays, axis=axis)


def split(value):
    high = value.astype(BF16)
    return high, (value - high.astype(F32)).astype(BF16)


def swap_groups(parts, width):
    parts = list(parts)
    lane = lax.broadcasted_iota(jnp.int32, parts[0].shape, 1)
    bit = len(parts) // 2
    while bit:
        shift = bit * width
        low = (lane // shift) % 2 == 0
        for at in range(len(parts)):
            if at & bit:
                continue
            a, b = parts[at], parts[at | bit]
            parts[at] = jnp.where(low, a, pltpu.roll(b, shift, 1))
            parts[at | bit] = jnp.where(low, pltpu.roll(a, LANES - shift, 1), b)
        bit //= 2
    return parts


def pack_wire(plan, total_ref, wire_ref):
    slot, group = plan.slot, plan.per_tile
    for half in range(plan.halves):
        for block in range(plan.groups):
            parts = [
                total_ref[pl.ds((block * group + j) * slot, slot), pl.ds(half * LANES, LANES)] for j in range(group)
            ]
            parts = swap_groups(parts, plan.width)
            owner_y, tile = block // plan.tiles, block % plan.tiles
            for g in range(group):
                target = (half * group + g) * plan.count_y + owner_y
                wire_ref[target, :, pl.ds(tile * LANES, LANES)] = parts[g].astype(BF16)


def unpack_wire(plan, load, spectrum_ref):
    slot, group = plan.slot, plan.per_tile
    for half in range(plan.halves):
        for block in range(plan.groups):
            owner_y, tile = block // plan.tiles, block % plan.tiles
            parts = [
                load((half * group + g) * plan.count_y + owner_y, pl.ds(tile * LANES, LANES)).astype(F32)
                for g in range(group)
            ]
            parts = swap_groups(parts, plan.width)
            for j in range(group):
                spectrum_ref[pl.ds((block * group + j) * slot, slot), pl.ds(half * LANES, LANES)] = parts[j].astype(BF16)


def blocks_of(wire_ref):
    return lambda device, lanes: wire_ref[device, :, lanes]


def synthesise(plan, load, second_t, third_t_ref, spectrum_ref, cells_ref):
    unpack_wire(plan, load, spectrum_ref)
    spectrum = spectrum_ref[...]
    inner = dot(second_t, spectrum).astype(BF16)
    cells_ref[...] = dot(inner, third_t_ref[...])


def piece_rows(plan, k):
    return pl.ds(pl.multiple_of(k * plan.piece, 16), plan.piece)


def each_piece(plan, flags, works, arriving=(), leaving=()):
    per_side = plan.pieces // plan.count_y
    for which in range(plan.count_y):
        for k in range(per_side):
            piece = (1 - flags[0] if which else flags[0]) * per_side + k
            rows = piece_rows(plan, piece)
            for ref, source, sems in arriving:
                pltpu.make_async_copy(source.at[:, rows], ref.at[:, rows], sems.at[piece]).wait()
            for work in works:

                def step(c, carry):
                    in_side = pl.ds(pl.multiple_of(k * plan.piece + c * CHUNK, 16), CHUNK)
                    work(which, in_side, pl.ds(pl.multiple_of(piece * plan.piece + c * CHUNK, 16), CHUNK))
                    return carry

                lax.fori_loop(0, plan.piece // CHUNK, step, 0)
            for ref, target, sems in leaving:
                pltpu.make_async_copy(ref.at[:, rows], target.at[:, rows], sems.at[piece]).start()


def start_pieces(plan, arriving):
    for k in range(plan.pieces):
        rows = piece_rows(plan, k)
        for ref, source, sems in arriving:
            pltpu.make_async_copy(source.at[:, rows], ref.at[:, rows], sems.at[k]).start()


def start_sides(plan, flags, own, other, target, sems):
    per_side = plan.pieces // plan.count_y
    for k in range(per_side):
        at = k * plan.piece
        there = pl.ds(pl.multiple_of(flags[0] * plan.side + at, 16), plan.piece)
        other_there = there if other.shape == own.shape else pl.ds(at, plan.piece)
        for half, source in [(flags[0], own.at[:, there]), (1 - flags[0], other.at[:, other_there])]:
            piece = half * per_side + k
            pltpu.make_async_copy(source, target.at[:, piece_rows(plan, piece)], sems.at[piece]).start()


def wait_pieces(plan, leaving):
    for ref, target, sems in leaving:
        for p in range(plan.pieces):
            rows = piece_rows(plan, p)
            pltpu.make_async_copy(ref.at[:, rows], target.at[:, rows], sems.at[p]).wait()


def sums_over_z(fields, third_ref):
    return dot(join([fields, fields], 1), join([third_ref[0], third_ref[1]], 0))


def finish(plan, sums, second_ref, total_ref, wire_ref):
    high, low = split(sums)
    total_ref[...] = dot(join([second_ref[0], second_ref[0], second_ref[1]], 1), join([high, low, high], 0))
    pack_wire(plan, total_ref, wire_ref)


def gelu_slope(value):
    size = jnp.abs(value)
    t = 1.0 / (1.0 + (0.3275911 * 0.7071067811865476) * size)
    poly = 0.5 * 1.061405429
    for c in (-1.453152027, 1.421413741, -0.284496736, 0.254829592):
        poly = poly * t + 0.5 * c
    bell = jnp.exp(-0.5 * value * value)
    tail = bell * (poly * t - 0.3989422804014327 * size)
    return jnp.where(value >= 0, 1.0 - tail, tail)


def each_chunk(total, chunk, work):
    def step(k, carry):
        work(pl.ds(pl.multiple_of(k * chunk, chunk), chunk))
        return carry

    lax.fori_loop(0, total // chunk, step, 0)


def lanes_of(plan, channel):
    return pl.ds(channel * plan.length_z, plan.length_z)


def mixed_with(plan, mixing_ref, values, out, transposed):
    total = None
    for k, value in enumerate(values):
        term = (mixing_ref[k, out] if transposed else mixing_ref[out, k]) * value
        total = term if total is None else total + term
    return total


def starts(copies, sems):
    copies = [pltpu.make_async_copy(source, target, sems.at[k]) for k, (source, target) in enumerate(copies)]
    for copy in copies:
        copy.start()
    return copies


def waits(copies):
    for copy in copies:
        copy.wait()


def own_side(plan, flags, k=0):
    at = flags[0] if k == 0 else 1 - flags[0]
    return pl.ds(pl.multiple_of(at * plan.side, 16), plan.side)


def position():
    return lax.axis_index("gy"), lax.axis_index("segment")


def input_own_kernel(
    plan, act_hbm, third_hbm, second_hbm, third_ref, second_ref, sums_ref, own_ref, sems
):
    flags = position()
    copies = starts(
        [(third_hbm, third_ref), (act_hbm.at[:, own_side(plan, flags)], own_ref), (second_hbm, second_ref)], sems
    )
    waits(copies[:2])
    sums_ref[...] = sums_over_z(join([own_ref[i] for i in range(plan.channels)], 1), third_ref)
    waits(copies[2:])


def input_kernel(
    plan, third_ref, second_ref, own_sums_ref, other_ref, mixing_ref, wire_ref, other_hbm, three_ref,
    sums_ref, total_ref, sems,
):
    flags = position()
    values = mixing_ref[...]
    three_ref[...] = jnp.zeros_like(three_ref)
    for k in range(3):
        part = values.astype(BF16)
        three_ref[0, :, pl.ds(k * values.shape[1], values.shape[1])] = part
        values = values - part.astype(F32)
    halves = [own_side(plan, flags, k) for k in range(2)]
    copies = starts([(other_ref, other_hbm)], sems)
    sums_ref[halves[0], :] = own_sums_ref[...]
    sums_ref[halves[1], :] = sums_over_z(join([other_ref[i] for i in range(plan.channels)], 1), third_ref)
    finish(plan, sums_ref[...], second_ref, total_ref, wire_ref)
    waits(copies)


def mix_inputs(plan, mixing_ref, act_ref, mixed_ref):
    def work(which, in_side, rows):
        inputs = [act_ref[i, rows, :].astype(F32) for i in range(plan.channels)]
        for o in range(plan.channels):
            mixed = mixed_with(plan, mixing_ref, inputs, o, False) + mixing_ref[o, plan.channels]
            mixed_ref[o, rows, :] = mixed

    return work


def first_kernel(
    plan, segments, flags, mixing_ref, act_hbm, act_other_hbm, cot_hbm, cot_other_hbm, third_hbm, second_hbm,
    wire_in_ref, third_t_ref, second_t_ref, wire_ref, kept_hbm,
    act_ref, cot_ref, kept_ref, third_ref, second_ref, total_ref, spectrum_ref, cells_ref, signals_ref, sems, piece_sems,
):
    last = flags[1] == segments - 1
    start_sides(plan, flags, act_hbm, act_other_hbm, act_ref, piece_sems.at[0])
    start_sides(plan, flags, cot_hbm, cot_other_hbm, cot_ref, piece_sems.at[1])
    copies = starts([(third_hbm, third_ref), (second_hbm, second_ref)], sems)
    synthesise(plan, blocks_of(wire_in_ref), second_t_ref[...], third_t_ref, spectrum_ref, cells_ref)
    arriving = [(act_ref, act_hbm, piece_sems.at[0]), (cot_ref, act_hbm, piece_sems.at[1])]
    leaving = [(kept_ref, kept_hbm, piece_sems.at[2])]
    mix = mix_inputs(plan, mixing_ref, act_ref, kept_ref)

    @pl.when(last)
    def _():
        def work(which, in_side, rows):
            for o in range(plan.channels):
                slope = gelu_slope(kept_ref[o, rows, :] + cells_ref[rows, lanes_of(plan, o)])
                signal = cot_ref[o, rows, :].astype(F32) * slope
                kept_ref[o, rows, :] = signal
                signals_ref[rows, lanes_of(plan, o)] = signal.astype(BF16)

        each_piece(plan, flags, [mix, work], arriving, leaving)
        waits(copies)
        finish(plan, sums_over_z(signals_ref[...], third_ref), second_ref, total_ref, wire_ref)

    @pl.when(jnp.logical_not(last))
    def _():
        def work(which, in_side, rows):
            for o in range(plan.channels):
                pre = kept_ref[o, rows, :] + cells_ref[rows, lanes_of(plan, o)]
                kept_ref[o, rows, :] = gelu_slope(pre)

        each_piece(plan, flags, [mix, work], arriving, leaving)
        waits(copies)

    wait_pieces(plan, leaving)


def shared_kernel(
    plan, segments, columns, flags, act_hbm, act_other_hbm, cot_hbm, cot_other_hbm, wire_hbm, third_t_ref,
    second_t_ref, local_ref, act_ref, cot_ref, wire_ref, spectrum_ref, cells_ref, values_ref, mixing_ref, sems,
    piece_sems,
):
    @pl.when(flags[1] == segments - 2)
    def _():
        copies = starts([(wire_hbm, wire_ref)], sems)
        start_sides(plan, flags, act_hbm, act_other_hbm, act_ref, piece_sems.at[0])
        start_sides(plan, flags, cot_hbm, cot_other_hbm, cot_ref, piece_sems.at[1])
        waits(copies)
        parts = [
            wire_ref[plan.devices, :, pl.ds(k * columns, columns)].astype(F32) for k in range(3)
        ]
        values_ref[:, pl.ds(0, columns)] = parts[0] + parts[1] + parts[2]
        copies = starts([(values_ref, mixing_ref)], sems)
        synthesise(plan, blocks_of(wire_ref), second_t_ref[...], third_t_ref, spectrum_ref, cells_ref)
        waits(copies)

        def slope(which, in_side, rows):
            for o in range(plan.channels):
                pre = local_ref[o, rows, :] + cells_ref[rows, lanes_of(plan, o)]
                local_ref[o, rows, :] = cot_ref[o, rows, :].astype(F32) * gelu_slope(pre)

        def back(which, in_side, rows):
            signals = [local_ref[o, rows, :] for o in range(plan.channels)]
            for i in range(plan.channels):
                local_ref[i, rows, :] = mixed_with(plan, mixing_ref, signals, i, True)

        arriving = [(act_ref, act_hbm, piece_sems.at[0]), (cot_ref, act_hbm, piece_sems.at[1])]
        each_piece(plan, flags, [mix_inputs(plan, mixing_ref, act_ref, local_ref), slope, back], arriving)


def middle_kernel(
    plan, segments, turn, flags, mixing_ref, kept_hbm, local_ref, wire_in_ref, third_ref, third_t_ref, second_ref,
    second_t_ref, wire_ref, local_out_ref,
    kept_ref, total_ref, spectrum_ref, cells_ref, signals_ref, sems, piece_sems,
):
    segment = flags[1]
    active = segments - 1 - turn
    kept = (kept_ref, kept_hbm, piece_sems.at[0])

    @pl.when(segment < active)
    def _():
        start_pieces(plan, [kept])
        synthesise(plan, lambda device, lanes: wire_in_ref[active * plan.devices + device, :, lanes],
                   second_t_ref[...], third_t_ref, spectrum_ref, cells_ref)

        def work(which, in_side, rows):
            signals = []
            for i in range(plan.channels):
                grad = local_ref[i, rows, :] + cells_ref[rows, lanes_of(plan, i)]
                signals.append(grad * kept_ref[i, rows, :])
                signals_ref[rows, lanes_of(plan, i)] = signals[i].astype(BF16)
            for i in range(plan.channels):
                local_out_ref[i, rows, :] = mixed_with(plan, mixing_ref, signals, i, True)

        each_piece(plan, flags, [work], [kept])
        finish(plan, sums_over_z(signals_ref[...], third_ref), second_ref, total_ref, wire_ref)

    @pl.when(segment >= active)
    def _():
        if turn == 0:
            start_pieces(plan, [kept])

            def work(which, in_side, rows):
                signals = [kept_ref[o, rows, :] for o in range(plan.channels)]
                for i in range(plan.channels):
                    local_out_ref[i, rows, :] = mixed_with(plan, mixing_ref, signals, i, True)

            each_piece(plan, flags, [work], [kept])
        else:
            waits(starts([(local_ref, local_out_ref)], sems))


def side_grads(plan, segments, which, flags, local_ref, third_t_ref, second_t_ref, wire_in_ref, kept_wire_ref,
               grad_ref, spectrum_ref, cells_ref):
    segment = flags[1]
    last = (segments - 1) * plan.devices
    here = own_side(plan, flags, which)

    def load(device, lanes):
        return jnp.where(segment == 0, wire_in_ref[device, :, lanes], kept_wire_ref[last + device, :, lanes])

    synthesise(plan, load, second_t_ref[here, :], third_t_ref, spectrum_ref, cells_ref)

    def work(rows):
        there = pl.ds(pl.multiple_of(rows.start + here.start, 16), rows.size)
        for i in range(plan.channels):
            grad_ref[i, rows, :] = (local_ref[i, there, :] + cells_ref[rows, lanes_of(plan, i)]).astype(BF16)

    each_chunk(plan.side, 64, work)


def last_other_kernel(
    plan, segments, local_ref, third_t_ref, second_t_ref, wire_in_ref, kept_wire_ref, grad_ref,
    spectrum_ref, cells_ref,
):
    flags = position()
    side_grads(plan, segments, 1, flags, local_ref, third_t_ref, second_t_ref, wire_in_ref, kept_wire_ref, grad_ref,
               spectrum_ref, cells_ref)


def last_own_kernel(
    plan, segments, local_ref, third_t_ref, second_t_ref, wire_in_ref, kept_wire_ref, input_modes_ref,
    modes_ref, kept_modes_ref, out_hbm, weight_hbm, spectrum_ref, cells_ref, weight_ref, grad_ref, sems,
):
    flags = position()
    modes = jnp.where(flags[1] == 0, modes_ref[...], kept_modes_ref[...])
    for i in range(plan.channels):
        weight_ref[:, i] = input_modes_ref[:, i : i + 1, :] * modes
    copies = starts([(weight_ref, weight_hbm)], sems)
    side_grads(plan, segments, 0, flags, local_ref, third_t_ref, second_t_ref, wire_in_ref, kept_wire_ref, grad_ref,
               spectrum_ref, cells_ref)
    waits(copies + starts([(grad_ref, out_hbm.at[:, own_side(plan, flags)])], sems.at[pl.ds(1, 1)]))


def nothing_kernel(unused, out_hbm):
    pass


def mode_sums(plan, wire_ref, first_ref):
    received = wire_ref[...].reshape(plan.devices * plan.slot, plan.lanes)
    sums = dot(first_ref[0], received) + dot(first_ref[1], received)
    modes = join([sums[p * MODES : (p + 1) * MODES].T for p in range(plan.parts)], 0)
    return modes.reshape(plan.modes, plan.channels, MODES)


def flatten(plan, mixed):
    rows = mixed.reshape(plan.parts, plan.lanes, MODES)
    return join([rows[p].T for p in range(plan.parts)], 0)


def mix_modes(plan, modes, weights_ref, backward):
    if not backward:
        mixed = weights_ref[:, 0] * modes[:, 0:1, :]
        for i in range(1, plan.channels):
            mixed = mixed + weights_ref[:, i] * modes[:, i : i + 1, :]
        return mixed
    row = lax.broadcasted_iota(jnp.int32, modes.shape, 1)
    mixed = jnp.zeros_like(modes)
    for i in range(plan.channels):
        mixed = jnp.where(row == i, jnp.sum(weights_ref[:, i] * modes, axis=1, keepdims=True), mixed)
    return mixed


def spread_modes(plan, mixed, first_t_ref):
    high, low = split(flatten(plan, mixed))
    spread = dot(first_t_ref[0], high) + dot(first_t_ref[0], low) + dot(first_t_ref[1], high)
    return spread.astype(BF16).reshape(plan.wire)


def spectral_kernel(plan, backward, wire_ref, weights_ref, first_ref, first_t_ref, modes_ref, wire_out_ref):
    modes = mode_sums(plan, wire_ref, first_ref)
    modes_ref[...] = modes
    spread = spread_modes(plan, mix_modes(plan, modes, weights_ref, backward), first_t_ref)
    copies = wire_out_ref.shape[0] // plan.devices
    for k in range(copies):
        wire_out_ref[pl.ds(k * plan.devices, plan.devices)] = spread


VMEM = pl.BlockSpec(memory_space=pltpu.VMEM)
SMEM = pl.BlockSpec(memory_space=pltpu.SMEM)
HBM = pl.BlockSpec(memory_space=pltpu.HBM)


def call(kernel, name, args, out_shape, scratch=(), scalars=0, far=0, aliases={}):
    specs = [SMEM] * scalars + [HBM] * far + [VMEM] * (len(args) - scalars - far)
    args = [
        pltpu.with_memory_space_constraint(arg, pltpu.HBM) if spec is HBM else arg for arg, spec in zip(args, specs)
    ]
    outs = out_shape if isinstance(out_shape, tuple) else (out_shape,)
    out_specs = tuple(HBM if getattr(out, "memory_space", None) is pltpu.HBM else VMEM for out in outs)
    result = pl.pallas_call(
        kernel, in_specs=specs, out_specs=out_specs, out_shape=outs, scratch_shapes=scratch,
        input_output_aliases=aliases,
        compiler_params=pltpu.CompilerParams(vmem_limit_bytes=VMEM_LIMIT), name=name,
    )(*args)
    return result if isinstance(out_shape, tuple) else result[0]


def exchange(wire, axes=PLANE):
    return lax.all_to_all(wire, axes, split_axis=0, concat_axis=0, tiled=True)


def from_behind(block, distance):
    devices = range(lax.axis_size("segment"))
    route = [(i - distance, i) for i in devices if i - distance in devices]
    return lax.ppermute(block, "segment", route)


def other_core(block):
    return lax.ppermute(block, "gy", [(0, 1), (1, 0)])


def body(activations, cotangent, spectral_weights, pointwise, channel_bias):
    _, channels, rows_x, rows_y, length_z = activations.shape
    plan = Plan(channels, rows_x, rows_y, length_z, lax.axis_size("gx"), lax.axis_size("gy"))
    act = activations.reshape(plan.field)
    cot = cotangent.reshape(plan.field)
    weights = spectral_weights.reshape(plan.modes, channels, channels, MODES)
    mixing = jnp.concatenate([pointwise[0], channel_bias[0][:, None]], axis=1)
    third, third_t = jnp.asarray(plan.third), jnp.asarray(plan.third_t)
    second, second_t = jnp.asarray(plan.second), jnp.asarray(plan.second_t)
    first, first_t = jnp.asarray(plan.first), jnp.asarray(plan.first_t)
    segment = lax.axis_index("segment")
    segments = lax.axis_size("segment")
    half = lax.axis_index("gy")

    wire_shape = jax.ShapeDtypeStruct(plan.wire, BF16)
    wires_shape = jax.ShapeDtypeStruct((segments * plan.devices,) + plan.wire[1:], BF16)
    modes_shape = jax.ShapeDtypeStruct((plan.modes, channels, MODES), F32)
    part_shape = (channels, plan.side, length_z)
    part = jax.ShapeDtypeStruct(part_shape, BF16)
    wide = pltpu.HBM(plan.field, F32)
    wide_scratch, narrow_scratch = pltpu.VMEM(plan.field, F32), pltpu.VMEM(plan.field, BF16)
    piece_sems = pltpu.SemaphoreType.DMA((3, plan.pieces))
    total = pltpu.VMEM(plan.spectrum, F32)
    spectrum = pltpu.VMEM(plan.spectrum, BF16)
    cells = pltpu.VMEM((plan.rows, channels * length_z), F32)
    half_cells = pltpu.VMEM((plan.side, channels * length_z), F32)
    signals = pltpu.VMEM((plan.rows, channels * length_z), BF16)
    flags = jnp.stack([half, segment])

    def sems(count):
        return pltpu.SemaphoreType.DMA((count,))

    def part_of(block, at):
        return lax.dynamic_slice_in_dim(block, at * plan.side, plan.side, 1)

    act_other = other_core(part_of(act, 1 - half))
    if segments > 1:
        act_next = from_behind(act, -1)
    parts = call(
        functools.partial(input_own_kernel, plan), "own_inputs", (act, third, second),
        (jax.ShapeDtypeStruct(third.shape, BF16), jax.ShapeDtypeStruct(second.shape, BF16),
         jax.ShapeDtypeStruct((plan.side, MODES * channels), F32)),
        [pltpu.VMEM(part_shape, BF16), sems(3)], 0, 3,
    )
    wire, act_other, in_three = call(
        functools.partial(input_kernel, plan), "input_modes",
        (*parts, act_other, jnp.pad(mixing, [(0, plan.slot - channels), (0, 0)])),
        (wire_shape, pltpu.HBM(part_shape, BF16), jax.ShapeDtypeStruct((1,) + plan.wire[1:], BF16)),
        [pltpu.VMEM((plan.rows, MODES * channels), F32), total, sems(2)],
    )
    cot_other = other_core(cot)
    input_modes, wire = call(
        functools.partial(spectral_kernel, plan, False), "mix_inputs", (exchange(wire), weights, first, first_t),
        (modes_shape, wire_shape),
    )
    wire_in = exchange(wire)
    if segments > 1:
        next_block = from_behind(jnp.concatenate([wire_in, in_three], axis=0), -1)
    wire, kept = call(
        functools.partial(first_kernel, plan, segments), "first_signal",
        (flags, mixing, act, act_other, cot, cot_other, third, second, wire_in, third_t, second_t), (wire_shape, wide),
        [narrow_scratch, narrow_scratch, wide_scratch, pltpu.VMEM(third.shape, BF16), pltpu.VMEM(second.shape, BF16),
         total, spectrum, cells, signals, sems(2), piece_sems], 2, 6,
    )

    def mix_signal(wire, count):
        return call(
            functools.partial(spectral_kernel, plan, True), "mix_signal", (wire, weights, first, first_t),
            (modes_shape, jax.ShapeDtypeStruct((count * plan.devices,) + plan.wire[1:], BF16)),
        )

    def of_last():
        return exchange(wire), call(nothing_kernel, "no_inputs", (flags,), pltpu.HBM(plan.field, BF16), scalars=1)

    def of_others():
        return wire, other_core(act_next)

    kept_wire = kept_modes = None
    for turn in range(segments - 1):
        active = segment == segments - 1 - turn
        if turn == 0:
            wire, next_other = lax.cond(active, of_last, of_others)
            wire, next_block = lax.optimization_barrier((wire, next_block))
            local = call(
                functools.partial(shared_kernel, plan, segments, mixing.shape[1]), "shared",
                (flags, act_next, next_other, cot, cot_other, next_block, third_t, second_t),
                jax.ShapeDtypeStruct(plan.field, F32),
                [narrow_scratch, narrow_scratch, pltpu.VMEM(next_block.shape, BF16), spectrum, cells,
                 pltpu.VMEM((plan.slot, LANES), F32), pltpu.SMEM((plan.slot, LANES), F32), sems(1), piece_sems], 1, 5,
            )
            wire, local = lax.optimization_barrier((wire, local))
        else:
            ahead = from_behind(local.astype(BF16), -1).astype(F32)
            local = jnp.where(segment == segments - 2 - turn, ahead, local)
            wire = exchange(wire)
        modes, wire = mix_signal(wire, segments)
        kept_modes = modes if kept_modes is None else jnp.where(active, modes, kept_modes)
        wires = exchange(wire, WHOLE)
        if kept_wire is None:
            kept_wire = wires
        else:
            here = lax.slice_in_dim(wires, (segments - 1 - turn) * plan.devices, (segments - turn) * plan.devices)
            old = lax.slice_in_dim(kept_wire, (segments - 1) * plan.devices, segments * plan.devices)
            kept_wire = jnp.concatenate(
                [kept_wire[: (segments - 1) * plan.devices], jnp.where(active, here, old)], axis=0
            )
        wire, local = call(
            functools.partial(middle_kernel, plan, segments, turn), "next_signal",
            (flags, mixing, kept, local, wires, third, third_t, second, second_t),
            (wire_shape, jax.ShapeDtypeStruct(plan.field, F32)),
            [wide_scratch, total, spectrum, cells, signals, sems(2), piece_sems], 2, 1,
        )
    if segments == 1:
        local = jnp.einsum("oi,oyz->iyz", pointwise[0], kept, precision=lax.Precision.HIGHEST)
    modes, wire = mix_signal(exchange(wire), 1)
    wire = exchange(wire)
    args = (local, third_t, second_t, wire, wire if kept_wire is None else kept_wire)
    weight_shape = (plan.modes, channels, channels, MODES)
    other_grads = call(
        functools.partial(last_other_kernel, plan, segments), "last_other", args, part, [spectrum, half_cells]
    )
    received = other_core(other_grads)
    grad, weight_grad = call(
        functools.partial(last_own_kernel, plan, segments), "last_own",
        args + (input_modes, modes, modes if kept_modes is None else kept_modes),
        (pltpu.HBM(plan.field, BF16), pltpu.HBM(weight_shape, F32)),
        [spectrum, half_cells, pltpu.VMEM(weight_shape, F32), pltpu.VMEM(part_shape, BF16), sems(2)],
    )
    grad = lax.dynamic_update_slice_in_dim(grad, received, (1 - half) * plan.side, 1)
    return grad.reshape(activations.shape), weight_grad.reshape(spectral_weights.shape)


def solution(mesh):
    return jax.shard_map(
        body,
        mesh=mesh,
        in_specs=(
            P("segment", "groups", "gx", "gy", None),
            P("groups", "gx", "gy", None),
            P("segment", "gy", "gx", None, None, None),
            P("segment", None, None),
            P("segment", None),
        ),
        out_specs=(
            P("segment", "groups", "gx", "gy", None),
            P("segment", "gy", "gx", "groups", None, None),
        ),
        check_vma=False,
    )
```

```python
import functools
import math

import jax
import jax.numpy as jnp
import ml_dtypes
import numpy as np
from jax import lax
from jax.experimental import pallas as pl
from jax.experimental.pallas import tpu as pltpu
from jax.sharding import PartitionSpec as P

MODES = 32
LANES = 128
PLANE = ("gy", "gx")
WHOLE = ("segment",) + PLANE
F32 = jnp.float32
BF16 = jnp.bfloat16
VMEM_LIMIT = 22 * 1024 * 1024
CHUNK = 64


def trig_basis(length):
    half = MODES // 2
    points = np.arange(length)[None, :]
    freqs = np.arange(half)[:, None]
    angle = 2.0 * math.pi / length
    rows = np.concatenate(
        [np.cos((freqs * points % length) * angle), np.sin(((freqs + 1) * points % length) * angle)], axis=0
    )
    scales = np.where(np.arange(MODES) == 0, 1.0 / math.sqrt(length), math.sqrt(2.0 / length))
    return rows * scales[:, None]


def high_low(values):
    high = values.astype(np.float32).astype(ml_dtypes.bfloat16)
    low = (values - high.astype(np.float64)).astype(np.float32).astype(ml_dtypes.bfloat16)
    return np.stack([high, low])


class Plan:
    def __init__(self, channels, rows_x, rows_y, length_z, count_x, count_y):
        self.channels, self.length_z = channels, length_z
        self.count_x, self.count_y = count_x, count_y
        self.devices = count_x * count_y
        share = rows_x // count_y
        self.side = share * rows_y
        self.rows = self.side * count_y
        self.pieces = 2 * count_y
        self.piece = self.rows // self.pieces
        self.own_third = MODES // count_x
        self.own_second = MODES // count_y
        self.width = self.own_third * channels
        self.parts = 2 if share <= 8 and self.own_second // 2 * self.width >= LANES else 1
        padded = 8 if self.parts == 2 else -(-share // 16) * 16
        self.in_part = self.own_second // self.parts
        self.slot = self.parts * padded
        self.per_tile = LANES // self.width
        self.tiles = self.in_part // self.per_tile
        self.groups = MODES // self.parts // self.per_tile
        self.halves = MODES * channels // LANES
        self.lanes = self.in_part * self.width
        self.wire = (self.devices, self.slot, self.lanes)
        self.modes = self.own_second * self.own_third
        self.spectrum = (MODES * padded, MODES * channels)
        self.field = (channels, self.rows, length_z)
        along_x = trig_basis(rows_x * count_x).reshape(MODES, count_x, count_y, share)
        along_x = np.swapaxes(along_x, 1, 2).reshape(MODES, self.devices, share)
        along_y = trig_basis(rows_y * count_y).reshape(MODES, count_y, rows_y)
        along_z = trig_basis(length_z)
        third = np.einsum("ik,cz->izck", np.eye(channels), along_z)
        third = third.reshape(channels * length_z, MODES * channels)
        self.third = high_low(third)
        self.third_t = high_low(third.T)[0]
        slabs = along_y.reshape(count_y, self.parts, self.in_part, count_y, rows_y)
        second = np.einsum("opqsy,xk->oqpxsky", slabs, np.eye(padded, share))
        second = second.reshape(MODES * padded, self.rows)
        self.second = high_low(second)
        self.second_t = high_low(second.T)[0]
        spread = np.zeros((MODES, self.devices, padded))
        spread[:, :, :share] = along_x
        first = np.einsum("pq,adx->padqx", np.eye(self.parts), spread)
        first = first.reshape(self.parts * MODES, self.devices * self.slot)
        self.first = high_low(first)
        self.first_t = high_low(first.T)


def dot(a, b):
    return jnp.dot(a, b, preferred_element_type=F32)


def join(arrays, axis):
    return jnp.concatenate(arrays, axis=axis)


def split(value):
    high = value.astype(BF16)
    return high, (value - high.astype(F32)).astype(BF16)


def swap_groups(parts, width):
    parts = list(parts)
    lane = lax.broadcasted_iota(jnp.int32, parts[0].shape, 1)
    bit = len(parts) // 2
    while bit:
        shift = bit * width
        low = (lane // shift) % 2 == 0
        for at in range(len(parts)):
            if at & bit:
                continue
            a, b = parts[at], parts[at | bit]
            parts[at] = jnp.where(low, a, pltpu.roll(b, shift, 1))
            parts[at | bit] = jnp.where(low, pltpu.roll(a, LANES - shift, 1), b)
        bit //= 2
    return parts


def pack_wire(plan, total_ref, wire_ref):
    slot, group = plan.slot, plan.per_tile
    for half in range(plan.halves):
        for block in range(plan.groups):
            parts = [
                total_ref[pl.ds((block * group + j) * slot, slot), pl.ds(half * LANES, LANES)] for j in range(group)
            ]
            parts = swap_groups(parts, plan.width)
            owner_y, tile = block // plan.tiles, block % plan.tiles
            for g in range(group):
                target = owner_y * plan.count_x + half * group + g
                wire_ref[target, :, pl.ds(tile * LANES, LANES)] = parts[g].astype(BF16)


def unpack_wire(plan, load, spectrum_ref):
    slot, group = plan.slot, plan.per_tile
    for half in range(plan.halves):
        for block in range(plan.groups):
            owner_y, tile = block // plan.tiles, block % plan.tiles
            parts = [
                load(owner_y * plan.count_x + half * group + g, pl.ds(tile * LANES, LANES)).astype(F32)
                for g in range(group)
            ]
            parts = swap_groups(parts, plan.width)
            for j in range(group):
                spectrum_ref[pl.ds((block * group + j) * slot, slot), pl.ds(half * LANES, LANES)] = parts[j].astype(BF16)


def blocks_of(wire_ref):
    return lambda device, lanes: wire_ref[device, :, lanes]


def synthesise(plan, load, second_t, third_t_ref, spectrum_ref, cells_ref):
    unpack_wire(plan, load, spectrum_ref)
    spectrum = spectrum_ref[...]
    inner = dot(second_t, spectrum).astype(BF16)
    cells_ref[...] = dot(inner, third_t_ref[...])


def piece_rows(plan, k):
    return pl.ds(pl.multiple_of(k * plan.piece, 16), plan.piece)


def each_piece(plan, flags, works, arriving=(), leaving=()):
    per_side = plan.pieces // plan.count_y
    for which in range(plan.count_y):
        for k in range(per_side):
            piece = (1 - flags[0] if which else flags[0]) * per_side + k
            rows = piece_rows(plan, piece)
            for ref, source, sems in arriving:
                pltpu.make_async_copy(source.at[:, rows], ref.at[:, rows], sems.at[piece]).wait()
            for work in works:

                def step(c, carry):
                    in_side = pl.ds(pl.multiple_of(k * plan.piece + c * CHUNK, 16), CHUNK)
                    work(which, in_side, pl.ds(pl.multiple_of(piece * plan.piece + c * CHUNK, 16), CHUNK))
                    return carry

                lax.fori_loop(0, plan.piece // CHUNK, step, 0)
            for ref, target, sems in leaving:
                pltpu.make_async_copy(ref.at[:, rows], target.at[:, rows], sems.at[piece]).start()


def start_pieces(plan, arriving):
    for k in range(plan.pieces):
        rows = piece_rows(plan, k)
        for ref, source, sems in arriving:
            pltpu.make_async_copy(source.at[:, rows], ref.at[:, rows], sems.at[k]).start()


def start_sides(plan, flags, arrays):
    per_side = plan.pieces // plan.count_y
    for which in range(plan.count_y):
        for k in range(per_side):
            at = k * plan.piece
            there = pl.ds(pl.multiple_of(flags[0] * plan.side + at, 16), plan.piece)
            piece = (1 - flags[0] if which else flags[0]) * per_side + k
            for own, other, target, sems in arrays:
                source = other if which else own
                if source.shape[1] == plan.side:
                    source = source.at[:, pl.ds(at, plan.piece)]
                else:
                    source = source.at[:, there]
                pltpu.make_async_copy(source, target.at[:, piece_rows(plan, piece)], sems.at[piece]).start()


def wait_pieces(plan, leaving):
    for ref, target, sems in leaving:
        for p in range(plan.pieces):
            rows = piece_rows(plan, p)
            pltpu.make_async_copy(ref.at[:, rows], target.at[:, rows], sems.at[p]).wait()


def sums_over_z(fields, third_ref):
    return dot(join([fields, fields], 1), join([third_ref[0], third_ref[1]], 0))


def finish(plan, sums, second_ref, total_ref, wire_ref):
    high, low = split(sums)
    total_ref[...] = dot(join([second_ref[0], second_ref[0], second_ref[1]], 1), join([high, low, high], 0))
    pack_wire(plan, total_ref, wire_ref)


def gelu_slope(value):
    size = jnp.abs(value)
    t = 1.0 / (1.0 + (0.3275911 * 0.7071067811865476) * size)
    poly = 0.5 * 1.061405429
    for c in (-1.453152027, 1.421413741, -0.284496736, 0.254829592):
        poly = poly * t + 0.5 * c
    bell = jnp.exp(-0.5 * value * value)
    tail = bell * (poly * t - 0.3989422804014327 * size)
    return jnp.where(value >= 0, 1.0 - tail, tail)


def each_chunk(total, chunk, work):
    def step(k, carry):
        work(pl.ds(pl.multiple_of(k * chunk, chunk), chunk))
        return carry

    lax.fori_loop(0, total // chunk, step, 0)


def lanes_of(plan, channel):
    return pl.ds(channel * plan.length_z, plan.length_z)


def mixed_with(plan, mixing_ref, values, out, transposed):
    total = None
    for k, value in enumerate(values):
        term = (mixing_ref[k, out] if transposed else mixing_ref[out, k]) * value
        total = term if total is None else total + term
    return total


def starts(copies, sems):
    copies = [pltpu.make_async_copy(source, target, sems.at[k]) for k, (source, target) in enumerate(copies)]
    for copy in copies:
        copy.start()
    return copies


def waits(copies):
    for copy in copies:
        copy.wait()


def own_side(plan, flags, k=0):
    at = flags[0] if k == 0 else 1 - flags[0]
    return pl.ds(pl.multiple_of(at * plan.side, 16), plan.side)


def position():
    return lax.axis_index("gy"), lax.axis_index("segment")


def input_own_kernel(
    plan, act_hbm, third_hbm, second_hbm, third_ref, second_ref, sums_ref, own_ref, sems
):
    flags = position()
    copies = starts(
        [(third_hbm, third_ref), (act_hbm.at[:, own_side(plan, flags)], own_ref), (second_hbm, second_ref)], sems
    )
    waits(copies[:2])
    sums_ref[...] = sums_over_z(join([own_ref[i] for i in range(plan.channels)], 1), third_ref)
    waits(copies[2:])


def input_kernel(
    plan, third_ref, second_ref, own_sums_ref, other_ref, mixing_ref, wire_ref, other_hbm, three_ref,
    sums_ref, total_ref, sems,
):
    flags = position()
    values = mixing_ref[...]
    three_ref[...] = jnp.zeros_like(three_ref)
    for k in range(3):
        part = values.astype(BF16)
        three_ref[0, :, pl.ds(k * values.shape[1], values.shape[1])] = part
        values = values - part.astype(F32)
    halves = [own_side(plan, flags, k) for k in range(2)]
    copies = starts([(other_ref, other_hbm)], sems)
    sums_ref[halves[0], :] = own_sums_ref[...]
    sums_ref[halves[1], :] = sums_over_z(join([other_ref[i] for i in range(plan.channels)], 1), third_ref)
    finish(plan, sums_ref[...], second_ref, total_ref, wire_ref)
    waits(copies)


def mix_inputs(plan, mixing_ref, act_ref, mixed_ref):
    def work(which, in_side, rows):
        inputs = [act_ref[i, rows, :].astype(F32) for i in range(plan.channels)]
        for o in range(plan.channels):
            mixed = mixed_with(plan, mixing_ref, inputs, o, False) + mixing_ref[o, plan.channels]
            mixed_ref[o, rows, :] = mixed

    return work


def first_kernel(
    plan, segments, flags, mixing_ref, act_hbm, act_other_hbm, cot_hbm, cot_other_hbm, third_hbm, second_hbm,
    wire_in_ref, third_t_ref, second_t_ref, wire_ref, kept_hbm,
    act_ref, cot_ref, kept_ref, third_ref, second_ref, total_ref, spectrum_ref, cells_ref, signals_ref, sems, piece_sems,
):
    last = flags[1] == segments - 1
    start_sides(plan, flags, [(act_hbm, act_other_hbm, act_ref, piece_sems.at[0]),
                              (cot_hbm, cot_other_hbm, cot_ref, piece_sems.at[1])])
    copies = starts([(third_hbm, third_ref), (second_hbm, second_ref)], sems)
    synthesise(plan, blocks_of(wire_in_ref), second_t_ref[...], third_t_ref, spectrum_ref, cells_ref)
    arriving = [(act_ref, act_hbm, piece_sems.at[0]), (cot_ref, act_hbm, piece_sems.at[1])]
    leaving = [(kept_ref, kept_hbm, piece_sems.at[2])]
    mix = mix_inputs(plan, mixing_ref, act_ref, kept_ref)

    @pl.when(last)
    def _():
        def work(which, in_side, rows):
            for o in range(plan.channels):
                slope = gelu_slope(kept_ref[o, rows, :] + cells_ref[rows, lanes_of(plan, o)])
                signal = cot_ref[o, rows, :].astype(F32) * slope
                kept_ref[o, rows, :] = signal
                signals_ref[rows, lanes_of(plan, o)] = signal.astype(BF16)

        each_piece(plan, flags, [mix, work], arriving, leaving)
        waits(copies)
        finish(plan, sums_over_z(signals_ref[...], third_ref), second_ref, total_ref, wire_ref)

    @pl.when(jnp.logical_not(last))
    def _():
        def work(which, in_side, rows):
            for o in range(plan.channels):
                pre = kept_ref[o, rows, :] + cells_ref[rows, lanes_of(plan, o)]
                kept_ref[o, rows, :] = gelu_slope(pre)

        each_piece(plan, flags, [mix, work], arriving, leaving)
        waits(copies)

    wait_pieces(plan, leaving)


def shared_kernel(
    plan, segments, columns, flags, act_hbm, act_other_hbm, cot_hbm, cot_other_hbm, wire_hbm, third_t_ref,
    second_t_ref, local_ref, act_ref, cot_ref, wire_ref, spectrum_ref, cells_ref, values_ref, mixing_ref, sems,
    piece_sems,
):
    @pl.when(flags[1] == segments - 2)
    def _():
        copies = starts([(wire_hbm, wire_ref)], sems)
        start_sides(plan, flags, [(act_hbm, act_other_hbm, act_ref, piece_sems.at[0]),
                                  (cot_hbm, cot_other_hbm, cot_ref, piece_sems.at[1])])
        waits(copies)
        parts = [
            wire_ref[plan.devices, :, pl.ds(k * columns, columns)].astype(F32) for k in range(3)
        ]
        values_ref[:, pl.ds(0, columns)] = parts[0] + parts[1] + parts[2]
        copies = starts([(values_ref, mixing_ref)], sems)
        synthesise(plan, blocks_of(wire_ref), second_t_ref[...], third_t_ref, spectrum_ref, cells_ref)
        waits(copies)

        def slope(which, in_side, rows):
            for o in range(plan.channels):
                pre = local_ref[o, rows, :] + cells_ref[rows, lanes_of(plan, o)]
                local_ref[o, rows, :] = cot_ref[o, rows, :].astype(F32) * gelu_slope(pre)

        def back(which, in_side, rows):
            signals = [local_ref[o, rows, :] for o in range(plan.channels)]
            for i in range(plan.channels):
                local_ref[i, rows, :] = mixed_with(plan, mixing_ref, signals, i, True)

        arriving = [(act_ref, act_hbm, piece_sems.at[0]), (cot_ref, act_hbm, piece_sems.at[1])]
        each_piece(plan, flags, [mix_inputs(plan, mixing_ref, act_ref, local_ref), slope, back], arriving)


def middle_kernel(
    plan, segments, turn, flags, mixing_ref, kept_hbm, local_ref, wire_in_ref, third_ref, third_t_ref, second_ref,
    second_t_ref, wire_ref, local_out_ref,
    kept_ref, total_ref, spectrum_ref, cells_ref, signals_ref, sems, piece_sems,
):
    segment = flags[1]
    active = segments - 1 - turn
    kept = (kept_ref, kept_hbm, piece_sems.at[0])

    @pl.when(segment < active)
    def _():
        start_pieces(plan, [kept])
        synthesise(plan, lambda device, lanes: wire_in_ref[active * plan.devices + device, :, lanes],
                   second_t_ref[...], third_t_ref, spectrum_ref, cells_ref)

        def work(which, in_side, rows):
            signals = []
            for i in range(plan.channels):
                grad = local_ref[i, rows, :] + cells_ref[rows, lanes_of(plan, i)]
                signals.append(grad * kept_ref[i, rows, :])
                signals_ref[rows, lanes_of(plan, i)] = signals[i].astype(BF16)
            for i in range(plan.channels):
                local_out_ref[i, rows, :] = mixed_with(plan, mixing_ref, signals, i, True)

        each_piece(plan, flags, [work], [kept])
        finish(plan, sums_over_z(signals_ref[...], third_ref), second_ref, total_ref, wire_ref)

    @pl.when(segment >= active)
    def _():
        if turn == 0:
            start_pieces(plan, [kept])

            def work(which, in_side, rows):
                signals = [kept_ref[o, rows, :] for o in range(plan.channels)]
                for i in range(plan.channels):
                    local_out_ref[i, rows, :] = mixed_with(plan, mixing_ref, signals, i, True)

            each_piece(plan, flags, [work], [kept])
        else:
            waits(starts([(local_ref, local_out_ref)], sems))


def side_grads(plan, segments, which, flags, local_ref, third_t_ref, second_t_ref, wire_in_ref, kept_wire_ref,
               grad_ref, spectrum_ref, cells_ref):
    segment = flags[1]
    last = (segments - 1) * plan.devices
    here = own_side(plan, flags, which)

    def load(device, lanes):
        return jnp.where(segment == 0, wire_in_ref[device, :, lanes], kept_wire_ref[last + device, :, lanes])

    synthesise(plan, load, second_t_ref[here, :], third_t_ref, spectrum_ref, cells_ref)

    def work(rows):
        there = pl.ds(pl.multiple_of(rows.start + here.start, 16), rows.size)
        for i in range(plan.channels):
            grad_ref[i, rows, :] = (local_ref[i, there, :] + cells_ref[rows, lanes_of(plan, i)]).astype(BF16)

    each_chunk(plan.side, 64, work)


def last_other_kernel(
    plan, segments, local_ref, third_t_ref, second_t_ref, wire_in_ref, kept_wire_ref, grad_ref,
    spectrum_ref, cells_ref,
):
    flags = position()
    side_grads(plan, segments, 1, flags, local_ref, third_t_ref, second_t_ref, wire_in_ref, kept_wire_ref, grad_ref,
               spectrum_ref, cells_ref)


def last_own_kernel(
    plan, segments, local_ref, third_t_ref, second_t_ref, wire_in_ref, kept_wire_ref, input_modes_ref,
    modes_ref, kept_modes_ref, out_hbm, weight_hbm, spectrum_ref, cells_ref, weight_ref, grad_ref, sems,
):
    flags = position()
    modes = jnp.where(flags[1] == 0, modes_ref[...], kept_modes_ref[...])
    for i in range(plan.channels):
        weight_ref[:, i] = input_modes_ref[:, i : i + 1, :] * modes
    copies = starts([(weight_ref, weight_hbm)], sems)
    side_grads(plan, segments, 0, flags, local_ref, third_t_ref, second_t_ref, wire_in_ref, kept_wire_ref, grad_ref,
               spectrum_ref, cells_ref)
    waits(copies + starts([(grad_ref, out_hbm.at[:, own_side(plan, flags)])], sems.at[pl.ds(1, 1)]))


def nothing_kernel(unused, out_hbm):
    pass


def mode_sums(plan, wire_ref, first_ref):
    received = wire_ref[...].reshape(plan.devices * plan.slot, plan.lanes)
    sums = dot(first_ref[0], received) + dot(first_ref[1], received)
    modes = join([sums[p * MODES : (p + 1) * MODES].T for p in range(plan.parts)], 0)
    return modes.reshape(plan.modes, plan.channels, MODES)


def flatten(plan, mixed):
    rows = mixed.reshape(plan.parts, plan.lanes, MODES)
    return join([rows[p].T for p in range(plan.parts)], 0)


def mix_modes(plan, modes, weights_ref, backward):
    if not backward:
        mixed = weights_ref[:, 0] * modes[:, 0:1, :]
        for i in range(1, plan.channels):
            mixed = mixed + weights_ref[:, i] * modes[:, i : i + 1, :]
        return mixed
    row = lax.broadcasted_iota(jnp.int32, modes.shape, 1)
    mixed = jnp.zeros_like(modes)
    for i in range(plan.channels):
        mixed = jnp.where(row == i, jnp.sum(weights_ref[:, i] * modes, axis=1, keepdims=True), mixed)
    return mixed


def spread_modes(plan, mixed, first_t_ref):
    high, low = split(flatten(plan, mixed))
    spread = dot(first_t_ref[0], high) + dot(first_t_ref[0], low) + dot(first_t_ref[1], high)
    return spread.astype(BF16).reshape(plan.wire)


def inputs_kernel(plan, wire_ref, weights_ref, first_ref, first_t_ref, modes_hbm, wire_out_ref, modes_ref, sems):
    modes = mode_sums(plan, wire_ref, first_ref)
    modes_ref[...] = modes
    copies = starts([(modes_ref, modes_hbm)], sems)
    wire_out_ref[...] = spread_modes(plan, mix_modes(plan, modes, weights_ref, False), first_t_ref)
    waits(copies)


def spectral_kernel(plan, wire_ref, weights_ref, first_ref, first_t_ref, modes_ref, wire_out_ref):
    modes = mode_sums(plan, wire_ref, first_ref)
    modes_ref[...] = modes
    spread = spread_modes(plan, mix_modes(plan, modes, weights_ref, True), first_t_ref)
    copies = wire_out_ref.shape[0] // plan.devices
    for k in range(copies):
        wire_out_ref[pl.ds(k * plan.devices, plan.devices)] = spread


VMEM = pl.BlockSpec(memory_space=pltpu.VMEM)
SMEM = pl.BlockSpec(memory_space=pltpu.SMEM)
HBM = pl.BlockSpec(memory_space=pltpu.HBM)


def call(kernel, name, args, out_shape, scratch=(), scalars=0, far=0, aliases={}):
    specs = [SMEM] * scalars + [HBM] * far + [VMEM] * (len(args) - scalars - far)
    args = [
        pltpu.with_memory_space_constraint(arg, pltpu.HBM) if spec is HBM else arg for arg, spec in zip(args, specs)
    ]
    outs = out_shape if isinstance(out_shape, tuple) else (out_shape,)
    out_specs = tuple(HBM if getattr(out, "memory_space", None) is pltpu.HBM else VMEM for out in outs)
    result = pl.pallas_call(
        kernel, in_specs=specs, out_specs=out_specs, out_shape=outs, scratch_shapes=scratch,
        input_output_aliases=aliases,
        compiler_params=pltpu.CompilerParams(vmem_limit_bytes=VMEM_LIMIT), name=name,
    )(*args)
    return result if isinstance(out_shape, tuple) else result[0]


def exchange(wire, axes=PLANE):
    return lax.all_to_all(wire, axes, split_axis=0, concat_axis=0, tiled=True)


def from_behind(block, distance):
    devices = range(lax.axis_size("segment"))
    route = [(i - distance, i) for i in devices if i - distance in devices]
    return lax.ppermute(block, "segment", route)


def other_core(block):
    return lax.ppermute(block, "gy", [(0, 1), (1, 0)])


def body(activations, cotangent, spectral_weights, pointwise, channel_bias):
    _, channels, rows_x, rows_y, length_z = activations.shape
    plan = Plan(channels, rows_x, rows_y, length_z, lax.axis_size("gx"), lax.axis_size("gy"))
    act = activations.reshape(plan.field)
    cot = cotangent.reshape(plan.field)
    weights = spectral_weights.reshape(plan.modes, channels, channels, MODES)
    mixing = jnp.concatenate([pointwise[0], channel_bias[0][:, None]], axis=1)
    third, third_t = jnp.asarray(plan.third), jnp.asarray(plan.third_t)
    second, second_t = jnp.asarray(plan.second), jnp.asarray(plan.second_t)
    first, first_t = jnp.asarray(plan.first), jnp.asarray(plan.first_t)
    segment = lax.axis_index("segment")
    segments = lax.axis_size("segment")
    half = lax.axis_index("gy")

    wire_shape = jax.ShapeDtypeStruct(plan.wire, BF16)
    wires_shape = jax.ShapeDtypeStruct((segments * plan.devices,) + plan.wire[1:], BF16)
    modes_shape = jax.ShapeDtypeStruct((plan.modes, channels, MODES), F32)
    part_shape = (channels, plan.side, length_z)
    part = jax.ShapeDtypeStruct(part_shape, BF16)
    wide = pltpu.HBM(plan.field, F32)
    wide_scratch, narrow_scratch = pltpu.VMEM(plan.field, F32), pltpu.VMEM(plan.field, BF16)
    piece_sems = pltpu.SemaphoreType.DMA((3, plan.pieces))
    total = pltpu.VMEM(plan.spectrum, F32)
    spectrum = pltpu.VMEM(plan.spectrum, BF16)
    cells = pltpu.VMEM((plan.rows, channels * length_z), F32)
    half_cells = pltpu.VMEM((plan.side, channels * length_z), F32)
    signals = pltpu.VMEM((plan.rows, channels * length_z), BF16)
    flags = jnp.stack([half, segment])

    def sems(count):
        return pltpu.SemaphoreType.DMA((count,))

    def part_of(block, at):
        return lax.dynamic_slice_in_dim(block, at * plan.side, plan.side, 1)

    act_other = other_core(part_of(act, 1 - half))
    if segments > 1:
        act_next = from_behind(act, -1)
    parts = call(
        functools.partial(input_own_kernel, plan), "own_inputs", (act, third, second),
        (jax.ShapeDtypeStruct(third.shape, BF16), jax.ShapeDtypeStruct(second.shape, BF16),
         jax.ShapeDtypeStruct((plan.side, MODES * channels), F32)),
        [pltpu.VMEM(part_shape, BF16), sems(3)], 0, 3,
    )
    wire, act_other, in_three = call(
        functools.partial(input_kernel, plan), "input_modes",
        (*parts, act_other, jnp.pad(mixing, [(0, plan.slot - channels), (0, 0)])),
        (wire_shape, pltpu.HBM(part_shape, BF16), jax.ShapeDtypeStruct((1,) + plan.wire[1:], BF16)),
        [pltpu.VMEM((plan.rows, MODES * channels), F32), total, sems(2)],
    )
    cot_other = other_core(cot)
    input_modes, wire = call(
        functools.partial(inputs_kernel, plan), "mix_inputs", (exchange(wire), weights, first, first_t),
        (pltpu.HBM(modes_shape.shape, F32), wire_shape), [pltpu.VMEM(modes_shape.shape, F32), sems(1)],
    )
    wire_in = exchange(wire)
    if segments > 1:
        next_block = from_behind(jnp.concatenate([wire_in, in_three], axis=0), -1)
    wire, kept = call(
        functools.partial(first_kernel, plan, segments), "first_signal",
        (flags, mixing, act, act_other, cot, cot_other, third, second, wire_in, third_t, second_t), (wire_shape, wide),
        [narrow_scratch, narrow_scratch, wide_scratch, pltpu.VMEM(third.shape, BF16), pltpu.VMEM(second.shape, BF16),
         total, spectrum, cells, signals, sems(2), piece_sems], 2, 6,
    )

    def mix_signal(wire, count):
        return call(
            functools.partial(spectral_kernel, plan), "mix_signal", (wire, weights, first, first_t),
            (modes_shape, jax.ShapeDtypeStruct((count * plan.devices,) + plan.wire[1:], BF16)),
        )

    def of_last():
        return exchange(wire), call(nothing_kernel, "no_inputs", (flags,), pltpu.HBM(plan.field, BF16), scalars=1)

    def of_others():
        return wire, other_core(act_next)

    kept_wire = kept_modes = None
    for turn in range(segments - 1):
        active = segment == segments - 1 - turn
        if turn == 0:
            wire, next_other = lax.cond(active, of_last, of_others)
            wire, next_block = lax.optimization_barrier((wire, next_block))
            local = call(
                functools.partial(shared_kernel, plan, segments, mixing.shape[1]), "shared",
                (flags, act_next, next_other, cot, cot_other, next_block, third_t, second_t),
                jax.ShapeDtypeStruct(plan.field, F32),
                [narrow_scratch, narrow_scratch, pltpu.VMEM(next_block.shape, BF16), spectrum, cells,
                 pltpu.VMEM((plan.slot, LANES), F32), pltpu.SMEM((plan.slot, LANES), F32), sems(1), piece_sems], 1, 5,
            )
            wire, local = lax.optimization_barrier((wire, local))
        else:
            ahead = from_behind(local.astype(BF16), -1).astype(F32)
            local = jnp.where(segment == segments - 2 - turn, ahead, local)
            wire = exchange(wire)
        modes, wire = mix_signal(wire, segments)
        kept_modes = modes if kept_modes is None else jnp.where(active, modes, kept_modes)
        wires = exchange(wire, WHOLE)
        if kept_wire is None:
            kept_wire = wires
        else:
            here = lax.slice_in_dim(wires, (segments - 1 - turn) * plan.devices, (segments - turn) * plan.devices)
            old = lax.slice_in_dim(kept_wire, (segments - 1) * plan.devices, segments * plan.devices)
            kept_wire = jnp.concatenate(
                [kept_wire[: (segments - 1) * plan.devices], jnp.where(active, here, old)], axis=0
            )
        wire, local = call(
            functools.partial(middle_kernel, plan, segments, turn), "next_signal",
            (flags, mixing, kept, local, wires, third, third_t, second, second_t),
            (wire_shape, jax.ShapeDtypeStruct(plan.field, F32)),
            [wide_scratch, total, spectrum, cells, signals, sems(2), piece_sems], 2, 1,
        )
    if segments == 1:
        local = jnp.einsum("oi,oyz->iyz", pointwise[0], kept, precision=lax.Precision.HIGHEST)
    modes, wire = mix_signal(exchange(wire), 1)
    wire = exchange(wire)
    args = (local, third_t, second_t, wire, wire if kept_wire is None else kept_wire)
    weight_shape = (plan.modes, channels, channels, MODES)
    other_grads = call(
        functools.partial(last_other_kernel, plan, segments), "last_other", args, part, [spectrum, half_cells]
    )
    received = other_core(other_grads)
    grad, weight_grad = call(
        functools.partial(last_own_kernel, plan, segments), "last_own",
        args + (input_modes, modes, modes if kept_modes is None else kept_modes),
        (pltpu.HBM(plan.field, BF16), pltpu.HBM(weight_shape, F32)),
        [spectrum, half_cells, pltpu.VMEM(weight_shape, F32), pltpu.VMEM(part_shape, BF16), sems(2)],
    )
    grad = lax.dynamic_update_slice_in_dim(grad, received, (1 - half) * plan.side, 1)
    return grad.reshape(activations.shape), weight_grad.reshape(spectral_weights.shape)


def solution(mesh):
    return jax.shard_map(
        body,
        mesh=mesh,
        in_specs=(
            P("segment", "groups", "gx", "gy", None),
            P("groups", "gx", "gy", None),
            P("segment", "gy", "gx", None, None, None),
            P("segment", None, None),
            P("segment", None),
        ),
        out_specs=(
            P("segment", "groups", "gx", "gy", None),
            P("segment", "gy", "gx", "groups", None, None),
        ),
        check_vma=False,
    )
```

```python
import functools
import math

import jax
import jax.numpy as jnp
import ml_dtypes
import numpy as np
from jax import lax
from jax.experimental import pallas as pl
from jax.experimental.pallas import tpu as pltpu
from jax.sharding import PartitionSpec as P

MODES = 32
LANES = 128
PLANE = ("gy", "gx")
WHOLE = ("segment",) + PLANE
F32 = jnp.float32
BF16 = jnp.bfloat16
VMEM_LIMIT = 22 * 1024 * 1024
CHUNK = 64


def trig_basis(length):
    half = MODES // 2
    points = np.arange(length)[None, :]
    freqs = np.arange(half)[:, None]
    angle = 2.0 * math.pi / length
    rows = np.concatenate(
        [np.cos((freqs * points % length) * angle), np.sin(((freqs + 1) * points % length) * angle)], axis=0
    )
    scales = np.where(np.arange(MODES) == 0, 1.0 / math.sqrt(length), math.sqrt(2.0 / length))
    return rows * scales[:, None]


def high_low(values):
    high = values.astype(np.float32).astype(ml_dtypes.bfloat16)
    low = (values - high.astype(np.float64)).astype(np.float32).astype(ml_dtypes.bfloat16)
    return np.stack([high, low])


class Plan:
    def __init__(self, channels, rows_x, rows_y, length_z, count_x, count_y):
        self.channels, self.length_z = channels, length_z
        self.count_x, self.count_y = count_x, count_y
        self.devices = count_x * count_y
        share = rows_x // count_y
        self.side = share * rows_y
        self.rows = self.side * count_y
        self.pieces = 2 * count_y
        self.piece = self.rows // self.pieces
        self.own_third = MODES // count_x
        self.own_second = MODES // count_y
        self.width = self.own_third * channels
        self.parts = 2 if share <= 8 and self.own_second // 2 * self.width >= LANES else 1
        padded = 8 if self.parts == 2 else -(-share // 16) * 16
        self.in_part = self.own_second // self.parts
        self.slot = self.parts * padded
        self.per_tile = LANES // self.width
        self.tiles = self.in_part // self.per_tile
        self.groups = MODES // self.parts // self.per_tile
        self.halves = MODES * channels // LANES
        self.lanes = self.in_part * self.width
        self.wire = (self.devices, self.slot, self.lanes)
        self.modes = self.own_second * self.own_third
        self.spectrum = (MODES * padded, MODES * channels)
        self.field = (channels, self.rows, length_z)
        along_x = trig_basis(rows_x * count_x).reshape(MODES, count_x, count_y, share)
        along_x = np.swapaxes(along_x, 1, 2).reshape(MODES, self.devices, share)
        along_y = trig_basis(rows_y * count_y).reshape(MODES, count_y, rows_y)
        along_z = trig_basis(length_z)
        third = np.einsum("ik,cz->izck", np.eye(channels), along_z)
        third = third.reshape(channels * length_z, MODES * channels)
        self.third = high_low(third)
        self.third_t = high_low(third.T)[0]
        slabs = along_y.reshape(count_y, self.parts, self.in_part, count_y, rows_y)
        second = np.einsum("opqsy,xk->oqpxsky", slabs, np.eye(padded, share))
        second = second.reshape(MODES * padded, self.rows)
        self.second = high_low(second)
        self.second_t = high_low(second.T)[0]
        spread = np.zeros((MODES, self.devices, padded))
        spread[:, :, :share] = along_x
        first = np.einsum("pq,adx->padqx", np.eye(self.parts), spread)
        first = first.reshape(self.parts * MODES, self.devices * self.slot)
        self.first = high_low(first)
        self.first_t = high_low(first.T)


def dot(a, b):
    return jnp.dot(a, b, preferred_element_type=F32)


def join(arrays, axis):
    return jnp.concatenate(arrays, axis=axis)


def split(value):
    high = value.astype(BF16)
    return high, (value - high.astype(F32)).astype(BF16)


def swap_groups(parts, width):
    parts = list(parts)
    lane = lax.broadcasted_iota(jnp.int32, parts[0].shape, 1)
    bit = len(parts) // 2
    while bit:
        shift = bit * width
        low = (lane // shift) % 2 == 0
        for at in range(len(parts)):
            if at & bit:
                continue
            a, b = parts[at], parts[at | bit]
            parts[at] = jnp.where(low, a, pltpu.roll(b, shift, 1))
            parts[at | bit] = jnp.where(low, pltpu.roll(a, LANES - shift, 1), b)
        bit //= 2
    return parts


def pack_wire(plan, total_ref, wire_ref):
    slot, group = plan.slot, plan.per_tile
    for half in range(plan.halves):
        for block in range(plan.groups):
            parts = [
                total_ref[pl.ds((block * group + j) * slot, slot), pl.ds(half * LANES, LANES)] for j in range(group)
            ]
            parts = swap_groups(parts, plan.width)
            owner_y, tile = block // plan.tiles, block % plan.tiles
            for g in range(group):
                target = owner_y * plan.count_x + half * group + g
                wire_ref[target, :, pl.ds(tile * LANES, LANES)] = parts[g].astype(BF16)


def unpack_wire(plan, load, spectrum_ref):
    slot, group = plan.slot, plan.per_tile
    for half in range(plan.halves):
        for block in range(plan.groups):
            owner_y, tile = block // plan.tiles, block % plan.tiles
            parts = [
                load(owner_y * plan.count_x + half * group + g, pl.ds(tile * LANES, LANES)).astype(F32)
                for g in range(group)
            ]
            parts = swap_groups(parts, plan.width)
            for j in range(group):
                spectrum_ref[pl.ds((block * group + j) * slot, slot), pl.ds(half * LANES, LANES)] = parts[j].astype(BF16)


def blocks_of(wire_ref):
    return lambda device, lanes: wire_ref[device, :, lanes]


def synthesise(plan, load, second_t, third_t_ref, spectrum_ref, cells_ref):
    unpack_wire(plan, load, spectrum_ref)
    spectrum = spectrum_ref[...]
    inner = dot(second_t, spectrum).astype(BF16)
    cells_ref[...] = dot(inner, third_t_ref[...])


def piece_rows(plan, k):
    return pl.ds(pl.multiple_of(k * plan.piece, 16), plan.piece)


def each_piece(plan, flags, works, arriving=(), leaving=()):
    per_side = plan.pieces // plan.count_y
    for which in range(plan.count_y):
        for k in range(per_side):
            piece = (1 - flags[0] if which else flags[0]) * per_side + k
            rows = piece_rows(plan, piece)
            for ref, source, sems in arriving:
                pltpu.make_async_copy(source.at[:, rows], ref.at[:, rows], sems.at[piece]).wait()
            for work in works:

                def step(c, carry):
                    in_side = pl.ds(pl.multiple_of(k * plan.piece + c * CHUNK, 16), CHUNK)
                    work(which, in_side, pl.ds(pl.multiple_of(piece * plan.piece + c * CHUNK, 16), CHUNK))
                    return carry

                lax.fori_loop(0, plan.piece // CHUNK, step, 0)
            for ref, target, sems in leaving:
                pltpu.make_async_copy(ref.at[:, rows], target.at[:, rows], sems.at[piece]).start()


def start_sides(plan, flags, arrays):
    per_side = plan.pieces // plan.count_y
    for which in range(plan.count_y):
        for k in range(per_side):
            at = k * plan.piece
            there = pl.ds(pl.multiple_of(flags[0] * plan.side + at, 16), plan.piece)
            piece = (1 - flags[0] if which else flags[0]) * per_side + k
            for own, other, target, sems in arrays:
                source = other if which else own
                if source.shape[1] == plan.side:
                    source = source.at[:, pl.ds(at, plan.piece)]
                else:
                    source = source.at[:, there]
                pltpu.make_async_copy(source, target.at[:, piece_rows(plan, piece)], sems.at[piece]).start()


def wait_pieces(plan, leaving):
    for ref, target, sems in leaving:
        for p in range(plan.pieces):
            rows = piece_rows(plan, p)
            pltpu.make_async_copy(ref.at[:, rows], target.at[:, rows], sems.at[p]).wait()


def sums_over_z(fields, third_ref):
    return dot(join([fields, fields], 1), join([third_ref[0], third_ref[1]], 0))


def finish(plan, sums, second_ref, total_ref, wire_ref):
    high, low = split(sums)
    total_ref[...] = dot(join([second_ref[0], second_ref[0], second_ref[1]], 1), join([high, low, high], 0))
    pack_wire(plan, total_ref, wire_ref)


def gelu_slope(value):
    size = jnp.abs(value)
    t = 1.0 / (1.0 + (0.3275911 * 0.7071067811865476) * size)
    poly = 0.5 * 1.061405429
    for c in (-1.453152027, 1.421413741, -0.284496736, 0.254829592):
        poly = poly * t + 0.5 * c
    bell = jnp.exp(-0.5 * value * value)
    tail = bell * (poly * t - 0.3989422804014327 * size)
    return jnp.where(value >= 0, 1.0 - tail, tail)


def each_chunk(total, chunk, work):
    def step(k, carry):
        work(pl.ds(pl.multiple_of(k * chunk, chunk), chunk))
        return carry

    lax.fori_loop(0, total // chunk, step, 0)


def lanes_of(plan, channel):
    return pl.ds(channel * plan.length_z, plan.length_z)


def mixed_with(plan, mixing_ref, values, out, transposed):
    total = None
    for k, value in enumerate(values):
        term = (mixing_ref[k, out] if transposed else mixing_ref[out, k]) * value
        total = term if total is None else total + term
    return total


def starts(copies, sems):
    copies = [pltpu.make_async_copy(source, target, sems.at[k]) for k, (source, target) in enumerate(copies)]
    for copy in copies:
        copy.start()
    return copies


def waits(copies):
    for copy in copies:
        copy.wait()


def own_side(plan, flags, k=0):
    at = flags[0] if k == 0 else 1 - flags[0]
    return pl.ds(pl.multiple_of(at * plan.side, 16), plan.side)


def position():
    return lax.axis_index("gy"), lax.axis_index("segment")


def input_own_kernel(
    plan, act_hbm, third_hbm, second_hbm, third_ref, second_ref, sums_ref, own_ref, sems
):
    flags = position()
    copies = starts(
        [(third_hbm, third_ref), (act_hbm.at[:, own_side(plan, flags)], own_ref), (second_hbm, second_ref)], sems
    )
    waits(copies[:2])
    sums_ref[...] = sums_over_z(join([own_ref[i] for i in range(plan.channels)], 1), third_ref)
    waits(copies[2:])


def input_kernel(
    plan, third_ref, second_ref, own_sums_ref, other_ref, mixing_ref, wire_ref, other_hbm, three_ref,
    sums_ref, total_ref, sems,
):
    flags = position()
    values = mixing_ref[...]
    three_ref[...] = jnp.zeros_like(three_ref)
    for k in range(3):
        part = values.astype(BF16)
        three_ref[0, :, pl.ds(k * values.shape[1], values.shape[1])] = part
        values = values - part.astype(F32)
    halves = [own_side(plan, flags, k) for k in range(2)]
    copies = starts([(other_ref, other_hbm)], sems)
    sums_ref[halves[0], :] = own_sums_ref[...]
    sums_ref[halves[1], :] = sums_over_z(join([other_ref[i] for i in range(plan.channels)], 1), third_ref)
    finish(plan, sums_ref[...], second_ref, total_ref, wire_ref)
    waits(copies)


def mix_inputs(plan, mixing_ref, act_ref, mixed_ref):
    def work(which, in_side, rows):
        inputs = [act_ref[i, rows, :].astype(F32) for i in range(plan.channels)]
        for o in range(plan.channels):
            mixed = mixed_with(plan, mixing_ref, inputs, o, False) + mixing_ref[o, plan.channels]
            mixed_ref[o, rows, :] = mixed

    return work


def first_kernel(
    plan, segments, flags, mixing_ref, act_hbm, act_other_hbm, cot_hbm, cot_other_hbm, third_hbm, second_hbm,
    wire_in_ref, third_t_ref, second_t_ref, wire_ref, kept_hbm,
    act_ref, cot_ref, kept_ref, third_ref, second_ref, total_ref, spectrum_ref, cells_ref, signals_ref, sems, piece_sems,
):
    last = flags[1] == segments - 1
    start_sides(plan, flags, [(act_hbm, act_other_hbm, act_ref, piece_sems.at[0]),
                              (cot_hbm, cot_other_hbm, cot_ref, piece_sems.at[1])])
    copies = starts([(third_hbm, third_ref), (second_hbm, second_ref)], sems)
    synthesise(plan, blocks_of(wire_in_ref), second_t_ref[...], third_t_ref, spectrum_ref, cells_ref)
    arriving = [(act_ref, act_hbm, piece_sems.at[0]), (cot_ref, act_hbm, piece_sems.at[1])]
    leaving = [(kept_ref, kept_hbm, piece_sems.at[2])]
    mix = mix_inputs(plan, mixing_ref, act_ref, kept_ref)

    @pl.when(last)
    def _():
        def work(which, in_side, rows):
            for o in range(plan.channels):
                slope = gelu_slope(kept_ref[o, rows, :] + cells_ref[rows, lanes_of(plan, o)])
                signal = cot_ref[o, rows, :].astype(F32) * slope
                kept_ref[o, rows, :] = signal
                signals_ref[rows, lanes_of(plan, o)] = signal.astype(BF16)

        each_piece(plan, flags, [mix, work], arriving, leaving)
        waits(copies)
        finish(plan, sums_over_z(signals_ref[...], third_ref), second_ref, total_ref, wire_ref)

    @pl.when(jnp.logical_not(last))
    def _():
        def work(which, in_side, rows):
            for o in range(plan.channels):
                pre = kept_ref[o, rows, :] + cells_ref[rows, lanes_of(plan, o)]
                kept_ref[o, rows, :] = gelu_slope(pre)

        each_piece(plan, flags, [mix, work], arriving, leaving)
        waits(copies)

    wait_pieces(plan, leaving)


def shared_kernel(
    plan, segments, columns, flags, act_hbm, act_other_hbm, cot_hbm, cot_other_hbm, wire_hbm, third_t_ref,
    second_t_ref, local_ref, act_ref, cot_ref, wire_ref, spectrum_ref, cells_ref, values_ref, mixing_ref, sems,
    piece_sems,
):
    @pl.when(flags[1] == segments - 2)
    def _():
        copies = starts([(wire_hbm, wire_ref)], sems)
        start_sides(plan, flags, [(act_hbm, act_other_hbm, act_ref, piece_sems.at[0]),
                                  (cot_hbm, cot_other_hbm, cot_ref, piece_sems.at[1])])
        waits(copies)
        parts = [
            wire_ref[plan.devices, :, pl.ds(k * columns, columns)].astype(F32) for k in range(3)
        ]
        values_ref[:, pl.ds(0, columns)] = parts[0] + parts[1] + parts[2]
        copies = starts([(values_ref, mixing_ref)], sems)
        synthesise(plan, blocks_of(wire_ref), second_t_ref[...], third_t_ref, spectrum_ref, cells_ref)
        waits(copies)

        def slope(which, in_side, rows):
            for o in range(plan.channels):
                pre = local_ref[o, rows, :] + cells_ref[rows, lanes_of(plan, o)]
                local_ref[o, rows, :] = cot_ref[o, rows, :].astype(F32) * gelu_slope(pre)

        def back(which, in_side, rows):
            signals = [local_ref[o, rows, :] for o in range(plan.channels)]
            for i in range(plan.channels):
                local_ref[i, rows, :] = mixed_with(plan, mixing_ref, signals, i, True)

        arriving = [(act_ref, act_hbm, piece_sems.at[0]), (cot_ref, act_hbm, piece_sems.at[1])]
        each_piece(plan, flags, [mix_inputs(plan, mixing_ref, act_ref, local_ref), slope, back], arriving)


def middle_kernel(
    plan, segments, turn, flags, mixing_ref, kept_ref, local_ref, wire_in_ref, third_ref, third_t_ref, second_ref,
    second_t_ref, wire_ref, local_out_ref,
    total_ref, spectrum_ref, cells_ref, signals_ref, sems,
):
    segment = flags[1]
    active = segments - 1 - turn

    @pl.when(segment < active)
    def _():
        synthesise(plan, lambda device, lanes: wire_in_ref[active * plan.devices + device, :, lanes],
                   second_t_ref[...], third_t_ref, spectrum_ref, cells_ref)

        def work(rows):
            signals = []
            for i in range(plan.channels):
                grad = local_ref[i, rows, :] + cells_ref[rows, lanes_of(plan, i)]
                signals.append(grad * kept_ref[i, rows, :])
                signals_ref[rows, lanes_of(plan, i)] = signals[i].astype(BF16)
            for i in range(plan.channels):
                local_out_ref[i, rows, :] = mixed_with(plan, mixing_ref, signals, i, True)

        each_chunk(plan.rows, CHUNK, work)
        finish(plan, sums_over_z(signals_ref[...], third_ref), second_ref, total_ref, wire_ref)

    @pl.when(segment >= active)
    def _():
        if turn == 0:
            def work(rows):
                signals = [kept_ref[o, rows, :] for o in range(plan.channels)]
                for i in range(plan.channels):
                    local_out_ref[i, rows, :] = mixed_with(plan, mixing_ref, signals, i, True)

            each_chunk(plan.rows, CHUNK, work)
        else:
            waits(starts([(local_ref, local_out_ref)], sems))


def side_grads(plan, segments, which, flags, local_ref, third_t_ref, second_t_ref, wire_in_ref, kept_wire_ref,
               grad_ref, spectrum_ref, cells_ref):
    segment = flags[1]
    last = (segments - 1) * plan.devices
    here = own_side(plan, flags, which)

    def load(device, lanes):
        return jnp.where(segment == 0, wire_in_ref[device, :, lanes], kept_wire_ref[last + device, :, lanes])

    synthesise(plan, load, second_t_ref[here, :], third_t_ref, spectrum_ref, cells_ref)

    def work(rows):
        there = pl.ds(pl.multiple_of(rows.start + here.start, 16), rows.size)
        for i in range(plan.channels):
            grad_ref[i, rows, :] = (local_ref[i, there, :] + cells_ref[rows, lanes_of(plan, i)]).astype(BF16)

    each_chunk(plan.side, 64, work)


def last_other_kernel(
    plan, segments, local_ref, third_t_ref, second_t_ref, wire_in_ref, kept_wire_ref, grad_ref,
    spectrum_ref, cells_ref,
):
    flags = position()
    side_grads(plan, segments, 1, flags, local_ref, third_t_ref, second_t_ref, wire_in_ref, kept_wire_ref, grad_ref,
               spectrum_ref, cells_ref)


def last_own_kernel(
    plan, segments, local_ref, third_t_ref, second_t_ref, wire_in_ref, kept_wire_ref, input_modes_ref,
    modes_ref, kept_modes_ref, out_hbm, weight_hbm, spectrum_ref, cells_ref, weight_ref, grad_ref, sems,
):
    flags = position()
    modes = jnp.where(flags[1] == 0, modes_ref[...], kept_modes_ref[...])
    for i in range(plan.channels):
        weight_ref[:, i] = input_modes_ref[:, i : i + 1, :] * modes
    copies = starts([(weight_ref, weight_hbm)], sems)
    side_grads(plan, segments, 0, flags, local_ref, third_t_ref, second_t_ref, wire_in_ref, kept_wire_ref, grad_ref,
               spectrum_ref, cells_ref)
    waits(copies + starts([(grad_ref, out_hbm.at[:, own_side(plan, flags)])], sems.at[pl.ds(1, 1)]))


def nothing_kernel(unused, out_hbm):
    pass


def mode_sums(plan, wire_ref, first_ref):
    received = wire_ref[...].reshape(plan.devices * plan.slot, plan.lanes)
    sums = dot(first_ref[0], received) + dot(first_ref[1], received)
    modes = join([sums[p * MODES : (p + 1) * MODES].T for p in range(plan.parts)], 0)
    return modes.reshape(plan.modes, plan.channels, MODES)


def flatten(plan, mixed):
    rows = mixed.reshape(plan.parts, plan.lanes, MODES)
    return join([rows[p].T for p in range(plan.parts)], 0)


def mix_modes(plan, modes, weights_ref, backward):
    if not backward:
        mixed = weights_ref[:, 0] * modes[:, 0:1, :]
        for i in range(1, plan.channels):
            mixed = mixed + weights_ref[:, i] * modes[:, i : i + 1, :]
        return mixed
    row = lax.broadcasted_iota(jnp.int32, modes.shape, 1)
    mixed = jnp.zeros_like(modes)
    for i in range(plan.channels):
        mixed = jnp.where(row == i, jnp.sum(weights_ref[:, i] * modes, axis=1, keepdims=True), mixed)
    return mixed


def spread_modes(plan, mixed, first_t_ref):
    high, low = split(flatten(plan, mixed))
    spread = dot(first_t_ref[0], high) + dot(first_t_ref[0], low) + dot(first_t_ref[1], high)
    return spread.astype(BF16).reshape(plan.wire)


def inputs_kernel(plan, wire_ref, weights_ref, first_ref, first_t_ref, modes_hbm, wire_out_ref, modes_ref, sems):
    modes = mode_sums(plan, wire_ref, first_ref)
    modes_ref[...] = modes
    copies = starts([(modes_ref, modes_hbm)], sems)
    wire_out_ref[...] = spread_modes(plan, mix_modes(plan, modes, weights_ref, False), first_t_ref)
    waits(copies)


def spectral_kernel(plan, wire_ref, weights_ref, first_ref, first_t_ref, modes_ref, wire_out_ref):
    modes = mode_sums(plan, wire_ref, first_ref)
    modes_ref[...] = modes
    spread = spread_modes(plan, mix_modes(plan, modes, weights_ref, True), first_t_ref)
    copies = wire_out_ref.shape[0] // plan.devices
    for k in range(copies):
        wire_out_ref[pl.ds(k * plan.devices, plan.devices)] = spread


VMEM = pl.BlockSpec(memory_space=pltpu.VMEM)
SMEM = pl.BlockSpec(memory_space=pltpu.SMEM)
HBM = pl.BlockSpec(memory_space=pltpu.HBM)


def call(kernel, name, args, out_shape, scratch=(), scalars=0, far=0, aliases={}):
    specs = [SMEM] * scalars + [HBM] * far + [VMEM] * (len(args) - scalars - far)
    args = [
        pltpu.with_memory_space_constraint(arg, pltpu.HBM) if spec is HBM else arg for arg, spec in zip(args, specs)
    ]
    outs = out_shape if isinstance(out_shape, tuple) else (out_shape,)
    out_specs = tuple(HBM if getattr(out, "memory_space", None) is pltpu.HBM else VMEM for out in outs)
    result = pl.pallas_call(
        kernel, in_specs=specs, out_specs=out_specs, out_shape=outs, scratch_shapes=scratch,
        input_output_aliases=aliases,
        compiler_params=pltpu.CompilerParams(vmem_limit_bytes=VMEM_LIMIT), name=name,
    )(*args)
    return result if isinstance(out_shape, tuple) else result[0]


def exchange(wire, axes=PLANE):
    return lax.all_to_all(wire, axes, split_axis=0, concat_axis=0, tiled=True)


def from_behind(block, distance):
    devices = range(lax.axis_size("segment"))
    route = [(i - distance, i) for i in devices if i - distance in devices]
    return lax.ppermute(block, "segment", route)


def other_core(block):
    return lax.ppermute(block, "gy", [(0, 1), (1, 0)])


def body(activations, cotangent, spectral_weights, pointwise, channel_bias):
    _, channels, rows_x, rows_y, length_z = activations.shape
    plan = Plan(channels, rows_x, rows_y, length_z, lax.axis_size("gx"), lax.axis_size("gy"))
    act = activations.reshape(plan.field)
    cot = cotangent.reshape(plan.field)
    weights = spectral_weights.reshape(plan.modes, channels, channels, MODES)
    mixing = jnp.concatenate([pointwise[0], channel_bias[0][:, None]], axis=1)
    third, third_t = jnp.asarray(plan.third), jnp.asarray(plan.third_t)
    second, second_t = jnp.asarray(plan.second), jnp.asarray(plan.second_t)
    first, first_t = jnp.asarray(plan.first), jnp.asarray(plan.first_t)
    segment = lax.axis_index("segment")
    segments = lax.axis_size("segment")
    half = lax.axis_index("gy")

    wire_shape = jax.ShapeDtypeStruct(plan.wire, BF16)
    wires_shape = jax.ShapeDtypeStruct((segments * plan.devices,) + plan.wire[1:], BF16)
    modes_shape = jax.ShapeDtypeStruct((plan.modes, channels, MODES), F32)
    part_shape = (channels, plan.side, length_z)
    part = jax.ShapeDtypeStruct(part_shape, BF16)
    wide = pltpu.HBM(plan.field, F32)
    wide_scratch, narrow_scratch = pltpu.VMEM(plan.field, F32), pltpu.VMEM(plan.field, BF16)
    piece_sems = pltpu.SemaphoreType.DMA((3, plan.pieces))
    total = pltpu.VMEM(plan.spectrum, F32)
    spectrum = pltpu.VMEM(plan.spectrum, BF16)
    cells = pltpu.VMEM((plan.rows, channels * length_z), F32)
    half_cells = pltpu.VMEM((plan.side, channels * length_z), F32)
    signals = pltpu.VMEM((plan.rows, channels * length_z), BF16)
    flags = jnp.stack([half, segment])

    def sems(count):
        return pltpu.SemaphoreType.DMA((count,))

    def part_of(block, at):
        return lax.dynamic_slice_in_dim(block, at * plan.side, plan.side, 1)

    act_other = other_core(part_of(act, 1 - half))
    if segments > 1:
        act_next = from_behind(act, -1)
    parts = call(
        functools.partial(input_own_kernel, plan), "own_inputs", (act, third, second),
        (jax.ShapeDtypeStruct(third.shape, BF16), jax.ShapeDtypeStruct(second.shape, BF16),
         jax.ShapeDtypeStruct((plan.side, MODES * channels), F32)),
        [pltpu.VMEM(part_shape, BF16), sems(3)], 0, 3,
    )
    wire, act_other, in_three = call(
        functools.partial(input_kernel, plan), "input_modes",
        (*parts, act_other, jnp.pad(mixing, [(0, plan.slot - channels), (0, 0)])),
        (wire_shape, pltpu.HBM(part_shape, BF16), jax.ShapeDtypeStruct((1,) + plan.wire[1:], BF16)),
        [pltpu.VMEM((plan.rows, MODES * channels), F32), total, sems(2)],
    )
    cot_other = other_core(cot)
    input_modes, wire = call(
        functools.partial(inputs_kernel, plan), "mix_inputs", (exchange(wire), weights, first, first_t),
        (pltpu.HBM(modes_shape.shape, F32), wire_shape), [pltpu.VMEM(modes_shape.shape, F32), sems(1)],
    )
    wire_in = exchange(wire)
    if segments > 1:
        next_block = from_behind(jnp.concatenate([wire_in, in_three], axis=0), -1)
    wire, kept = call(
        functools.partial(first_kernel, plan, segments), "first_signal",
        (flags, mixing, act, act_other, cot, cot_other, third, second, wire_in, third_t, second_t), (wire_shape, wide),
        [narrow_scratch, narrow_scratch, wide_scratch, pltpu.VMEM(third.shape, BF16), pltpu.VMEM(second.shape, BF16),
         total, spectrum, cells, signals, sems(2), piece_sems], 2, 6,
    )

    def mix_signal(wire, count):
        return call(
            functools.partial(spectral_kernel, plan), "mix_signal", (wire, weights, first, first_t),
            (modes_shape, jax.ShapeDtypeStruct((count * plan.devices,) + plan.wire[1:], BF16)),
        )

    def of_last():
        return exchange(wire), call(nothing_kernel, "no_inputs", (flags,), pltpu.HBM(plan.field, BF16), scalars=1)

    def of_others():
        return wire, other_core(act_next)

    kept_wire = kept_modes = None
    for turn in range(segments - 1):
        active = segment == segments - 1 - turn
        if turn == 0:
            wire, next_other = lax.cond(active, of_last, of_others)
            wire, next_block = lax.optimization_barrier((wire, next_block))
            local = call(
                functools.partial(shared_kernel, plan, segments, mixing.shape[1]), "shared",
                (flags, act_next, next_other, cot, cot_other, next_block, third_t, second_t),
                jax.ShapeDtypeStruct(plan.field, F32),
                [narrow_scratch, narrow_scratch, pltpu.VMEM(next_block.shape, BF16), spectrum, cells,
                 pltpu.VMEM((plan.slot, LANES), F32), pltpu.SMEM((plan.slot, LANES), F32), sems(1), piece_sems], 1, 5,
            )
            wire, local = lax.optimization_barrier((wire, local))
        else:
            ahead = from_behind(local.astype(BF16), -1).astype(F32)
            local = jnp.where(segment == segments - 2 - turn, ahead, local)
            wire = exchange(wire)
        modes, wire = mix_signal(wire, segments)
        kept_modes = modes if kept_modes is None else jnp.where(active, modes, kept_modes)
        wires = exchange(wire, WHOLE)
        if kept_wire is None:
            kept_wire = wires
        else:
            here = lax.slice_in_dim(wires, (segments - 1 - turn) * plan.devices, (segments - turn) * plan.devices)
            old = lax.slice_in_dim(kept_wire, (segments - 1) * plan.devices, segments * plan.devices)
            kept_wire = jnp.concatenate(
                [kept_wire[: (segments - 1) * plan.devices], jnp.where(active, here, old)], axis=0
            )
        wire, local = call(
            functools.partial(middle_kernel, plan, segments, turn), "next_signal",
            (flags, mixing, kept, local, wires, third, third_t, second, second_t),
            (wire_shape, jax.ShapeDtypeStruct(plan.field, F32)),
            [total, spectrum, cells, signals, sems(2)], 2,
        )
    if segments == 1:
        local = jnp.einsum("oi,oyz->iyz", pointwise[0], kept, precision=lax.Precision.HIGHEST)
    modes, wire = mix_signal(exchange(wire), 1)
    wire = exchange(wire)
    args = (local, third_t, second_t, wire, wire if kept_wire is None else kept_wire)
    weight_shape = (plan.modes, channels, channels, MODES)
    other_grads = call(
        functools.partial(last_other_kernel, plan, segments), "last_other", args, part, [spectrum, half_cells]
    )
    received = other_core(other_grads)
    grad, weight_grad = call(
        functools.partial(last_own_kernel, plan, segments), "last_own",
        args + (input_modes, modes, modes if kept_modes is None else kept_modes),
        (pltpu.HBM(plan.field, BF16), pltpu.HBM(weight_shape, F32)),
        [spectrum, half_cells, pltpu.VMEM(weight_shape, F32), pltpu.VMEM(part_shape, BF16), sems(2)],
    )
    grad = lax.dynamic_update_slice_in_dim(grad, received, (1 - half) * plan.side, 1)
    return grad.reshape(activations.shape), weight_grad.reshape(spectral_weights.shape)


def solution(mesh):
    return jax.shard_map(
        body,
        mesh=mesh,
        in_specs=(
            P("segment", "groups", "gx", "gy", None),
            P("groups", "gx", "gy", None),
            P("segment", "gy", "gx", None, None, None),
            P("segment", None, None),
            P("segment", None),
        ),
        out_specs=(
            P("segment", "groups", "gx", "gy", None),
            P("segment", "gy", "gx", "groups", None, None),
        ),
        check_vma=False,
    )
```

```python
import functools
import math

import jax
import jax.numpy as jnp
import ml_dtypes
import numpy as np
from jax import lax
from jax.experimental import pallas as pl
from jax.experimental.pallas import tpu as pltpu
from jax.sharding import PartitionSpec as P

MODES = 32
LANES = 128
PLANE = ("gy", "gx")
WHOLE = ("segment",) + PLANE
F32 = jnp.float32
BF16 = jnp.bfloat16
VMEM_LIMIT = 22 * 1024 * 1024
CHUNK = 64


def trig_basis(length):
    half = MODES // 2
    points = np.arange(length)[None, :]
    freqs = np.arange(half)[:, None]
    angle = 2.0 * math.pi / length
    rows = np.concatenate(
        [np.cos((freqs * points % length) * angle), np.sin(((freqs + 1) * points % length) * angle)], axis=0
    )
    scales = np.where(np.arange(MODES) == 0, 1.0 / math.sqrt(length), math.sqrt(2.0 / length))
    return rows * scales[:, None]


def high_low(values):
    high = values.astype(np.float32).astype(ml_dtypes.bfloat16)
    low = (values - high.astype(np.float64)).astype(np.float32).astype(ml_dtypes.bfloat16)
    return np.stack([high, low])


class Plan:
    def __init__(self, channels, rows_x, rows_y, length_z, count_x, count_y):
        self.channels, self.length_z = channels, length_z
        self.count_x, self.count_y = count_x, count_y
        self.devices = count_x * count_y
        share = rows_x // count_y
        self.side = share * rows_y
        self.rows = self.side * count_y
        self.pieces = 2 * count_y
        self.piece = self.rows // self.pieces
        self.own_third = MODES // count_x
        self.own_second = MODES // count_y
        self.width = self.own_third * channels
        self.parts = 2 if share <= 8 and self.own_second // 2 * self.width >= LANES else 1
        padded = 8 if self.parts == 2 else -(-share // 16) * 16
        self.in_part = self.own_second // self.parts
        self.slot = self.parts * padded
        self.per_tile = LANES // self.width
        self.tiles = self.in_part // self.per_tile
        self.groups = MODES // self.parts // self.per_tile
        self.halves = MODES * channels // LANES
        self.lanes = self.in_part * self.width
        self.wire = (self.devices, self.slot, self.lanes)
        self.modes = self.own_second * self.own_third
        self.spectrum = (MODES * padded, MODES * channels)
        self.field = (channels, self.rows, length_z)
        along_x = trig_basis(rows_x * count_x).reshape(MODES, count_x, count_y, share)
        along_x = np.swapaxes(along_x, 1, 2).reshape(MODES, self.devices, share)
        along_y = trig_basis(rows_y * count_y).reshape(MODES, count_y, rows_y)
        along_z = trig_basis(length_z)
        third = np.einsum("ik,cz->izck", np.eye(channels), along_z)
        third = third.reshape(channels * length_z, MODES * channels)
        self.third = high_low(third)
        self.third_t = high_low(third.T)[0]
        slabs = along_y.reshape(count_y, self.parts, self.in_part, count_y, rows_y)
        second = np.einsum("opqsy,xk->oqpxsky", slabs, np.eye(padded, share))
        second = second.reshape(MODES * padded, self.rows)
        self.second = high_low(second)
        self.second_t = high_low(second.T)[0]
        spread = np.zeros((MODES, self.devices, padded))
        spread[:, :, :share] = along_x
        first = np.einsum("pq,adx->padqx", np.eye(self.parts), spread)
        first = first.reshape(self.parts * MODES, self.devices * self.slot)
        self.first = high_low(first)
        self.first_t = high_low(first.T)


def dot(a, b):
    return jnp.dot(a, b, preferred_element_type=F32)


def join(arrays, axis):
    return jnp.concatenate(arrays, axis=axis)


def split(value):
    high = value.astype(BF16)
    return high, (value - high.astype(F32)).astype(BF16)


def swap_groups(parts, width):
    parts = list(parts)
    lane = lax.broadcasted_iota(jnp.int32, parts[0].shape, 1)
    bit = len(parts) // 2
    while bit:
        shift = bit * width
        low = (lane // shift) % 2 == 0
        for at in range(len(parts)):
            if at & bit:
                continue
            a, b = parts[at], parts[at | bit]
            parts[at] = jnp.where(low, a, pltpu.roll(b, shift, 1))
            parts[at | bit] = jnp.where(low, pltpu.roll(a, LANES - shift, 1), b)
        bit //= 2
    return parts


def pack_wire(plan, total_ref, wire_ref):
    slot, group = plan.slot, plan.per_tile
    for half in range(plan.halves):
        for block in range(plan.groups):
            parts = [
                total_ref[pl.ds((block * group + j) * slot, slot), pl.ds(half * LANES, LANES)] for j in range(group)
            ]
            parts = swap_groups(parts, plan.width)
            owner_y, tile = block // plan.tiles, block % plan.tiles
            for g in range(group):
                target = owner_y * plan.count_x + half * group + g
                wire_ref[target, :, pl.ds(tile * LANES, LANES)] = parts[g].astype(BF16)


def unpack_wire(plan, load, spectrum_ref):
    slot, group = plan.slot, plan.per_tile
    for half in range(plan.halves):
        for block in range(plan.groups):
            owner_y, tile = block // plan.tiles, block % plan.tiles
            parts = [
                load(owner_y * plan.count_x + half * group + g, pl.ds(tile * LANES, LANES)).astype(F32)
                for g in range(group)
            ]
            parts = swap_groups(parts, plan.width)
            for j in range(group):
                spectrum_ref[pl.ds((block * group + j) * slot, slot), pl.ds(half * LANES, LANES)] = parts[j].astype(BF16)


def blocks_of(wire_ref):
    return lambda device, lanes: wire_ref[device, :, lanes]


def synthesise(plan, load, second_t, third_t_ref, spectrum_ref, cells_ref):
    unpack_wire(plan, load, spectrum_ref)
    spectrum = spectrum_ref[...]
    inner = dot(second_t, spectrum).astype(BF16)
    cells_ref[...] = dot(inner, third_t_ref[...])


def piece_rows(plan, k):
    return pl.ds(pl.multiple_of(k * plan.piece, 16), plan.piece)


def each_piece(plan, flags, works, arriving=(), leaving=()):
    per_side = plan.pieces // plan.count_y
    for which in range(plan.count_y):
        for k in range(per_side):
            piece = (1 - flags[0] if which else flags[0]) * per_side + k
            rows = piece_rows(plan, piece)
            for ref, source, sems in arriving:
                pltpu.make_async_copy(source.at[:, rows], ref.at[:, rows], sems.at[piece]).wait()
            for work in works:

                def step(c, carry):
                    in_side = pl.ds(pl.multiple_of(k * plan.piece + c * CHUNK, 16), CHUNK)
                    work(which, in_side, pl.ds(pl.multiple_of(piece * plan.piece + c * CHUNK, 16), CHUNK))
                    return carry

                lax.fori_loop(0, plan.piece // CHUNK, step, 0)
            for ref, target, sems in leaving:
                pltpu.make_async_copy(ref.at[:, rows], target.at[:, rows], sems.at[piece]).start()


def start_pieces(plan, arriving):
    for k in range(plan.pieces):
        rows = piece_rows(plan, k)
        for ref, source, sems in arriving:
            pltpu.make_async_copy(source.at[:, rows], ref.at[:, rows], sems.at[k]).start()


def start_sides(plan, flags, arrays):
    per_side = plan.pieces // plan.count_y
    for which in range(plan.count_y):
        for k in range(per_side):
            at = k * plan.piece
            there = pl.ds(pl.multiple_of(flags[0] * plan.side + at, 16), plan.piece)
            piece = (1 - flags[0] if which else flags[0]) * per_side + k
            for own, other, target, sems in arrays:
                source = other if which else own
                if source.shape[1] == plan.side:
                    source = source.at[:, pl.ds(at, plan.piece)]
                else:
                    source = source.at[:, there]
                pltpu.make_async_copy(source, target.at[:, piece_rows(plan, piece)], sems.at[piece]).start()


def wait_pieces(plan, leaving):
    for ref, target, sems in leaving:
        for p in range(plan.pieces):
            rows = piece_rows(plan, p)
            pltpu.make_async_copy(ref.at[:, rows], target.at[:, rows], sems.at[p]).wait()


def sums_over_z(fields, third_ref):
    return dot(join([fields, fields], 1), join([third_ref[0], third_ref[1]], 0))


def finish(plan, sums, second_ref, total_ref, wire_ref):
    high, low = split(sums)
    total_ref[...] = dot(join([second_ref[0], second_ref[0], second_ref[1]], 1), join([high, low, high], 0))
    pack_wire(plan, total_ref, wire_ref)


def gelu_slope(value):
    size = jnp.abs(value)
    t = 1.0 / (1.0 + (0.3275911 * 0.7071067811865476) * size)
    poly = 0.5 * 1.061405429
    for c in (-1.453152027, 1.421413741, -0.284496736, 0.254829592):
        poly = poly * t + 0.5 * c
    bell = jnp.exp(-0.5 * value * value)
    tail = bell * (poly * t - 0.3989422804014327 * size)
    return jnp.where(value >= 0, 1.0 - tail, tail)


def each_chunk(total, chunk, work):
    def step(k, carry):
        work(pl.ds(pl.multiple_of(k * chunk, chunk), chunk))
        return carry

    lax.fori_loop(0, total // chunk, step, 0)


def lanes_of(plan, channel):
    return pl.ds(channel * plan.length_z, plan.length_z)


def mixed_with(plan, mixing_ref, values, out, transposed):
    total = None
    for k, value in enumerate(values):
        term = (mixing_ref[k, out] if transposed else mixing_ref[out, k]) * value
        total = term if total is None else total + term
    return total


def starts(copies, sems):
    copies = [pltpu.make_async_copy(source, target, sems.at[k]) for k, (source, target) in enumerate(copies)]
    for copy in copies:
        copy.start()
    return copies


def waits(copies):
    for copy in copies:
        copy.wait()


def own_side(plan, flags, k=0):
    at = flags[0] if k == 0 else 1 - flags[0]
    return pl.ds(pl.multiple_of(at * plan.side, 16), plan.side)


def position():
    return lax.axis_index("gy"), lax.axis_index("segment")


def input_own_kernel(
    plan, act_hbm, third_hbm, second_hbm, third_ref, second_ref, sums_ref, own_ref, sems
):
    flags = position()
    copies = starts(
        [(third_hbm, third_ref), (act_hbm.at[:, own_side(plan, flags)], own_ref), (second_hbm, second_ref)], sems
    )
    waits(copies[:2])
    sums_ref[...] = sums_over_z(join([own_ref[i] for i in range(plan.channels)], 1), third_ref)
    waits(copies[2:])


def input_kernel(
    plan, third_ref, second_ref, own_sums_ref, other_ref, mixing_ref, wire_ref, other_hbm, three_ref,
    sums_ref, total_ref, sems,
):
    flags = position()
    values = mixing_ref[...]
    three_ref[...] = jnp.zeros_like(three_ref)
    for k in range(3):
        part = values.astype(BF16)
        three_ref[0, :, pl.ds(k * values.shape[1], values.shape[1])] = part
        values = values - part.astype(F32)
    halves = [own_side(plan, flags, k) for k in range(2)]
    copies = starts([(other_ref, other_hbm)], sems)
    sums_ref[halves[0], :] = own_sums_ref[...]
    sums_ref[halves[1], :] = sums_over_z(join([other_ref[i] for i in range(plan.channels)], 1), third_ref)
    finish(plan, sums_ref[...], second_ref, total_ref, wire_ref)
    waits(copies)


def mix_inputs(plan, mixing_ref, act_ref, mixed_ref):
    def work(which, in_side, rows):
        inputs = [act_ref[i, rows, :].astype(F32) for i in range(plan.channels)]
        for o in range(plan.channels):
            mixed = mixed_with(plan, mixing_ref, inputs, o, False) + mixing_ref[o, plan.channels]
            mixed_ref[o, rows, :] = mixed

    return work


def first_kernel(
    plan, segments, flags, mixing_ref, act_hbm, act_other_hbm, cot_hbm, cot_other_hbm, third_hbm, second_hbm,
    wire_in_ref, third_t_ref, second_t_ref, wire_ref, kept_hbm,
    act_ref, cot_ref, kept_ref, third_ref, second_ref, total_ref, spectrum_ref, cells_ref, signals_ref, sems, piece_sems,
):
    last = flags[1] == segments - 1
    start_sides(plan, flags, [(act_hbm, act_other_hbm, act_ref, piece_sems.at[0]),
                              (cot_hbm, cot_other_hbm, cot_ref, piece_sems.at[1])])
    copies = starts([(third_hbm, third_ref), (second_hbm, second_ref)], sems)
    synthesise(plan, blocks_of(wire_in_ref), second_t_ref[...], third_t_ref, spectrum_ref, cells_ref)
    arriving = [(act_ref, act_hbm, piece_sems.at[0]), (cot_ref, act_hbm, piece_sems.at[1])]
    leaving = [(kept_ref, kept_hbm, piece_sems.at[2])]
    mix = mix_inputs(plan, mixing_ref, act_ref, kept_ref)

    @pl.when(last)
    def _():
        def work(which, in_side, rows):
            for o in range(plan.channels):
                slope = gelu_slope(kept_ref[o, rows, :] + cells_ref[rows, lanes_of(plan, o)])
                signal = cot_ref[o, rows, :].astype(F32) * slope
                kept_ref[o, rows, :] = signal
                signals_ref[rows, lanes_of(plan, o)] = signal.astype(BF16)

        each_piece(plan, flags, [mix, work], arriving, leaving)
        waits(copies)
        finish(plan, sums_over_z(signals_ref[...], third_ref), second_ref, total_ref, wire_ref)

    @pl.when(jnp.logical_not(last))
    def _():
        def work(which, in_side, rows):
            for o in range(plan.channels):
                pre = kept_ref[o, rows, :] + cells_ref[rows, lanes_of(plan, o)]
                kept_ref[o, rows, :] = gelu_slope(pre)

        each_piece(plan, flags, [mix, work], arriving, leaving)
        waits(copies)

    wait_pieces(plan, leaving)


def shared_kernel(
    plan, segments, columns, flags, act_hbm, act_other_hbm, cot_hbm, cot_other_hbm, wire_hbm, third_t_ref,
    second_t_ref, local_ref, act_ref, cot_ref, wire_ref, spectrum_ref, cells_ref, values_ref, mixing_ref, sems,
    piece_sems,
):
    @pl.when(flags[1] == segments - 2)
    def _():
        copies = starts([(wire_hbm, wire_ref)], sems)
        start_sides(plan, flags, [(act_hbm, act_other_hbm, act_ref, piece_sems.at[0]),
                                  (cot_hbm, cot_other_hbm, cot_ref, piece_sems.at[1])])
        waits(copies)
        parts = [
            wire_ref[plan.devices, :, pl.ds(k * columns, columns)].astype(F32) for k in range(3)
        ]
        values_ref[:, pl.ds(0, columns)] = parts[0] + parts[1] + parts[2]
        copies = starts([(values_ref, mixing_ref)], sems)
        synthesise(plan, blocks_of(wire_ref), second_t_ref[...], third_t_ref, spectrum_ref, cells_ref)
        waits(copies)

        def slope(which, in_side, rows):
            for o in range(plan.channels):
                pre = local_ref[o, rows, :] + cells_ref[rows, lanes_of(plan, o)]
                local_ref[o, rows, :] = cot_ref[o, rows, :].astype(F32) * gelu_slope(pre)

        def back(which, in_side, rows):
            signals = [local_ref[o, rows, :] for o in range(plan.channels)]
            for i in range(plan.channels):
                local_ref[i, rows, :] = mixed_with(plan, mixing_ref, signals, i, True)

        arriving = [(act_ref, act_hbm, piece_sems.at[0]), (cot_ref, act_hbm, piece_sems.at[1])]
        each_piece(plan, flags, [mix_inputs(plan, mixing_ref, act_ref, local_ref), slope, back], arriving)


def middle_kernel(
    plan, segments, turn, flags, mixing_ref, kept_hbm, local_ref, wire_in_ref, third_ref, third_t_ref, second_ref,
    second_t_ref, wire_ref, local_out_ref,
    kept_ref, total_ref, spectrum_ref, cells_ref, signals_ref, sems, piece_sems,
):
    segment = flags[1]
    active = segments - 1 - turn
    kept = (kept_ref, kept_hbm, piece_sems.at[0])

    @pl.when(segment < active)
    def _():
        start_pieces(plan, [kept])
        synthesise(plan, lambda device, lanes: wire_in_ref[active * plan.devices + device, :, lanes],
                   second_t_ref[...], third_t_ref, spectrum_ref, cells_ref)

        def work(which, in_side, rows):
            signals = []
            for i in range(plan.channels):
                grad = local_ref[i, rows, :] + cells_ref[rows, lanes_of(plan, i)]
                signals.append(grad * kept_ref[i, rows, :])
                signals_ref[rows, lanes_of(plan, i)] = signals[i].astype(BF16)
            for i in range(plan.channels):
                local_out_ref[i, rows, :] = mixed_with(plan, mixing_ref, signals, i, True)

        each_piece(plan, flags, [work], [kept])
        finish(plan, sums_over_z(signals_ref[...], third_ref), second_ref, total_ref, wire_ref)

    @pl.when(segment >= active)
    def _():
        if turn == 0:
            start_pieces(plan, [kept])

            def work(which, in_side, rows):
                signals = [kept_ref[o, rows, :] for o in range(plan.channels)]
                for i in range(plan.channels):
                    local_out_ref[i, rows, :] = mixed_with(plan, mixing_ref, signals, i, True)

            each_piece(plan, flags, [work], [kept])
        else:
            waits(starts([(local_ref, local_out_ref)], sems))


def side_grads(plan, segments, which, flags, local_ref, third_t_ref, second_t_ref, wire_in_ref, kept_wire_ref,
               grad_ref, spectrum_ref, cells_ref):
    segment = flags[1]
    last = (segments - 1) * plan.devices
    here = own_side(plan, flags, which)

    def load(device, lanes):
        return jnp.where(segment == 0, wire_in_ref[device, :, lanes], kept_wire_ref[last + device, :, lanes])

    synthesise(plan, load, second_t_ref[here, :], third_t_ref, spectrum_ref, cells_ref)

    def work(rows):
        there = pl.ds(pl.multiple_of(rows.start + here.start, 16), rows.size)
        for i in range(plan.channels):
            grad_ref[i, rows, :] = (local_ref[i, there, :] + cells_ref[rows, lanes_of(plan, i)]).astype(BF16)

    each_chunk(plan.side, 64, work)


def last_other_kernel(
    plan, segments, local_ref, third_t_ref, second_t_ref, wire_in_ref, kept_wire_ref, grad_ref,
    spectrum_ref, cells_ref,
):
    flags = position()
    side_grads(plan, segments, 1, flags, local_ref, third_t_ref, second_t_ref, wire_in_ref, kept_wire_ref, grad_ref,
               spectrum_ref, cells_ref)


def last_own_kernel(
    plan, segments, local_ref, third_t_ref, second_t_ref, wire_in_ref, kept_wire_ref, input_modes_ref,
    modes_ref, kept_modes_ref, out_hbm, weight_hbm, spectrum_ref, cells_ref, weight_ref, grad_ref, sems,
):
    flags = position()
    modes = jnp.where(flags[1] == 0, modes_ref[...], kept_modes_ref[...])
    for i in range(plan.channels):
        weight_ref[:, i] = input_modes_ref[:, i : i + 1, :] * modes
    copies = starts([(weight_ref, weight_hbm)], sems)
    side_grads(plan, segments, 0, flags, local_ref, third_t_ref, second_t_ref, wire_in_ref, kept_wire_ref, grad_ref,
               spectrum_ref, cells_ref)
    waits(copies + starts([(grad_ref, out_hbm.at[:, own_side(plan, flags)])], sems.at[pl.ds(1, 1)]))


def nothing_kernel(unused, out_hbm):
    pass


def mode_sums(plan, wire_ref, first_ref):
    received = wire_ref[...].reshape(plan.devices * plan.slot, plan.lanes)
    sums = dot(first_ref[0], received) + dot(first_ref[1], received)
    modes = join([sums[p * MODES : (p + 1) * MODES].T for p in range(plan.parts)], 0)
    return modes.reshape(plan.modes, plan.channels, MODES)


def flatten(plan, mixed):
    rows = mixed.reshape(plan.parts, plan.lanes, MODES)
    return join([rows[p].T for p in range(plan.parts)], 0)


def mix_modes(plan, modes, weights_ref, backward):
    if not backward:
        mixed = weights_ref[:, 0] * modes[:, 0:1, :]
        for i in range(1, plan.channels):
            mixed = mixed + weights_ref[:, i] * modes[:, i : i + 1, :]
        return mixed
    row = lax.broadcasted_iota(jnp.int32, modes.shape, 1)
    count = plan.channels
    terms = [weights_ref[:, i] * modes for i in range(count)]
    while len(terms) > 1:
        half = len(terms) // 2
        low = row // half % 2 == 0
        pairs = []
        for a, b in zip(terms[:half], terms[half:]):
            kept, moved = jnp.where(low, a, b), jnp.where(low, b, a)
            pairs.append(kept + jnp.where(low, pltpu.roll(moved, count - half, 1), pltpu.roll(moved, half, 1)))
        terms = pairs
    return terms[0]


def spread_modes(plan, mixed, first_t_ref):
    high, low = split(flatten(plan, mixed))
    spread = dot(first_t_ref[0], high) + dot(first_t_ref[0], low) + dot(first_t_ref[1], high)
    return spread.astype(BF16).reshape(plan.wire)


def inputs_kernel(plan, wire_ref, weights_ref, first_ref, first_t_ref, modes_hbm, wire_out_ref, modes_ref, sems):
    modes = mode_sums(plan, wire_ref, first_ref)
    modes_ref[...] = modes
    copies = starts([(modes_ref, modes_hbm)], sems)
    wire_out_ref[...] = spread_modes(plan, mix_modes(plan, modes, weights_ref, False), first_t_ref)
    waits(copies)


def spectral_kernel(plan, wire_ref, weights_ref, first_ref, first_t_ref, modes_ref, wire_out_ref):
    modes = mode_sums(plan, wire_ref, first_ref)
    modes_ref[...] = modes
    spread = spread_modes(plan, mix_modes(plan, modes, weights_ref, True), first_t_ref)
    copies = wire_out_ref.shape[0] // plan.devices
    for k in range(copies):
        wire_out_ref[pl.ds(k * plan.devices, plan.devices)] = spread


VMEM = pl.BlockSpec(memory_space=pltpu.VMEM)
SMEM = pl.BlockSpec(memory_space=pltpu.SMEM)
HBM = pl.BlockSpec(memory_space=pltpu.HBM)


def call(kernel, name, args, out_shape, scratch=(), scalars=0, far=0, aliases={}):
    specs = [SMEM] * scalars + [HBM] * far + [VMEM] * (len(args) - scalars - far)
    args = [
        pltpu.with_memory_space_constraint(arg, pltpu.HBM) if spec is HBM else arg for arg, spec in zip(args, specs)
    ]
    outs = out_shape if isinstance(out_shape, tuple) else (out_shape,)
    out_specs = tuple(HBM if getattr(out, "memory_space", None) is pltpu.HBM else VMEM for out in outs)
    result = pl.pallas_call(
        kernel, in_specs=specs, out_specs=out_specs, out_shape=outs, scratch_shapes=scratch,
        input_output_aliases=aliases,
        compiler_params=pltpu.CompilerParams(vmem_limit_bytes=VMEM_LIMIT), name=name,
    )(*args)
    return result if isinstance(out_shape, tuple) else result[0]


def exchange(wire, axes=PLANE):
    return lax.all_to_all(wire, axes, split_axis=0, concat_axis=0, tiled=True)


def from_behind(block, distance):
    devices = range(lax.axis_size("segment"))
    route = [(i - distance, i) for i in devices if i - distance in devices]
    return lax.ppermute(block, "segment", route)


def other_core(block):
    return lax.ppermute(block, "gy", [(0, 1), (1, 0)])


def body(activations, cotangent, spectral_weights, pointwise, channel_bias):
    _, channels, rows_x, rows_y, length_z = activations.shape
    plan = Plan(channels, rows_x, rows_y, length_z, lax.axis_size("gx"), lax.axis_size("gy"))
    act = activations.reshape(plan.field)
    cot = cotangent.reshape(plan.field)
    weights = spectral_weights.reshape(plan.modes, channels, channels, MODES)
    mixing = jnp.concatenate([pointwise[0], channel_bias[0][:, None]], axis=1)
    third, third_t = jnp.asarray(plan.third), jnp.asarray(plan.third_t)
    second, second_t = jnp.asarray(plan.second), jnp.asarray(plan.second_t)
    first, first_t = jnp.asarray(plan.first), jnp.asarray(plan.first_t)
    segment = lax.axis_index("segment")
    segments = lax.axis_size("segment")
    half = lax.axis_index("gy")

    wire_shape = jax.ShapeDtypeStruct(plan.wire, BF16)
    wires_shape = jax.ShapeDtypeStruct((segments * plan.devices,) + plan.wire[1:], BF16)
    modes_shape = jax.ShapeDtypeStruct((plan.modes, channels, MODES), F32)
    part_shape = (channels, plan.side, length_z)
    part = jax.ShapeDtypeStruct(part_shape, BF16)
    wide = pltpu.HBM(plan.field, F32)
    wide_scratch, narrow_scratch = pltpu.VMEM(plan.field, F32), pltpu.VMEM(plan.field, BF16)
    piece_sems = pltpu.SemaphoreType.DMA((3, plan.pieces))
    total = pltpu.VMEM(plan.spectrum, F32)
    spectrum = pltpu.VMEM(plan.spectrum, BF16)
    cells = pltpu.VMEM((plan.rows, channels * length_z), F32)
    half_cells = pltpu.VMEM((plan.side, channels * length_z), F32)
    signals = pltpu.VMEM((plan.rows, channels * length_z), BF16)
    flags = jnp.stack([half, segment])

    def sems(count):
        return pltpu.SemaphoreType.DMA((count,))

    def part_of(block, at):
        return lax.dynamic_slice_in_dim(block, at * plan.side, plan.side, 1)

    act_other = other_core(part_of(act, 1 - half))
    if segments > 1:
        act_next = from_behind(act, -1)
    parts = call(
        functools.partial(input_own_kernel, plan), "own_inputs", (act, third, second),
        (jax.ShapeDtypeStruct(third.shape, BF16), jax.ShapeDtypeStruct(second.shape, BF16),
         jax.ShapeDtypeStruct((plan.side, MODES * channels), F32)),
        [pltpu.VMEM(part_shape, BF16), sems(3)], 0, 3,
    )
    wire, act_other, in_three = call(
        functools.partial(input_kernel, plan), "input_modes",
        (*parts, act_other, jnp.pad(mixing, [(0, plan.slot - channels), (0, 0)])),
        (wire_shape, pltpu.HBM(part_shape, BF16), jax.ShapeDtypeStruct((1,) + plan.wire[1:], BF16)),
        [pltpu.VMEM((plan.rows, MODES * channels), F32), total, sems(2)],
    )
    cot_other = other_core(cot)
    input_modes, wire = call(
        functools.partial(inputs_kernel, plan), "mix_inputs", (exchange(wire), weights, first, first_t),
        (pltpu.HBM(modes_shape.shape, F32), wire_shape), [pltpu.VMEM(modes_shape.shape, F32), sems(1)],
    )
    wire_in = exchange(wire)
    if segments > 1:
        next_block = from_behind(jnp.concatenate([wire_in, in_three], axis=0), -1)
    wire, kept = call(
        functools.partial(first_kernel, plan, segments), "first_signal",
        (flags, mixing, act, act_other, cot, cot_other, third, second, wire_in, third_t, second_t), (wire_shape, wide),
        [narrow_scratch, narrow_scratch, wide_scratch, pltpu.VMEM(third.shape, BF16), pltpu.VMEM(second.shape, BF16),
         total, spectrum, cells, signals, sems(2), piece_sems], 2, 6,
    )

    def mix_signal(wire, count):
        return call(
            functools.partial(spectral_kernel, plan), "mix_signal", (wire, weights, first, first_t),
            (modes_shape, jax.ShapeDtypeStruct((count * plan.devices,) + plan.wire[1:], BF16)),
        )

    def of_last():
        return exchange(wire), call(nothing_kernel, "no_inputs", (flags,), pltpu.HBM(plan.field, BF16), scalars=1)

    def of_others():
        return wire, other_core(act_next)

    kept_wire = kept_modes = None
    for turn in range(segments - 1):
        active = segment == segments - 1 - turn
        if turn == 0:
            wire, next_other = lax.cond(active, of_last, of_others)
            wire, next_block = lax.optimization_barrier((wire, next_block))
            local = call(
                functools.partial(shared_kernel, plan, segments, mixing.shape[1]), "shared",
                (flags, act_next, next_other, cot, cot_other, next_block, third_t, second_t),
                jax.ShapeDtypeStruct(plan.field, F32),
                [narrow_scratch, narrow_scratch, pltpu.VMEM(next_block.shape, BF16), spectrum, cells,
                 pltpu.VMEM((plan.slot, LANES), F32), pltpu.SMEM((plan.slot, LANES), F32), sems(1), piece_sems], 1, 5,
            )
            wire, local = lax.optimization_barrier((wire, local))
        else:
            ahead = from_behind(local.astype(BF16), -1).astype(F32)
            local = jnp.where(segment == segments - 2 - turn, ahead, local)
            wire = exchange(wire)
        modes, wire = mix_signal(wire, segments)
        kept_modes = modes if kept_modes is None else jnp.where(active, modes, kept_modes)
        wires = exchange(wire, WHOLE)
        if kept_wire is None:
            kept_wire = wires
        else:
            here = lax.slice_in_dim(wires, (segments - 1 - turn) * plan.devices, (segments - turn) * plan.devices)
            old = lax.slice_in_dim(kept_wire, (segments - 1) * plan.devices, segments * plan.devices)
            kept_wire = jnp.concatenate(
                [kept_wire[: (segments - 1) * plan.devices], jnp.where(active, here, old)], axis=0
            )
        wire, local = call(
            functools.partial(middle_kernel, plan, segments, turn), "next_signal",
            (flags, mixing, kept, local, wires, third, third_t, second, second_t),
            (wire_shape, jax.ShapeDtypeStruct(plan.field, F32)),
            [wide_scratch, total, spectrum, cells, signals, sems(2), piece_sems], 2, 1,
        )
    if segments == 1:
        local = jnp.einsum("oi,oyz->iyz", pointwise[0], kept, precision=lax.Precision.HIGHEST)
    modes, wire = mix_signal(exchange(wire), 1)
    wire = exchange(wire)
    args = (local, third_t, second_t, wire, wire if kept_wire is None else kept_wire)
    weight_shape = (plan.modes, channels, channels, MODES)
    other_grads = call(
        functools.partial(last_other_kernel, plan, segments), "last_other", args, part, [spectrum, half_cells]
    )
    received = other_core(other_grads)
    grad, weight_grad = call(
        functools.partial(last_own_kernel, plan, segments), "last_own",
        args + (input_modes, modes, modes if kept_modes is None else kept_modes),
        (pltpu.HBM(plan.field, BF16), pltpu.HBM(weight_shape, F32)),
        [spectrum, half_cells, pltpu.VMEM(weight_shape, F32), pltpu.VMEM(part_shape, BF16), sems(2)],
    )
    grad = lax.dynamic_update_slice_in_dim(grad, received, (1 - half) * plan.side, 1)
    return grad.reshape(activations.shape), weight_grad.reshape(spectral_weights.shape)


def solution(mesh):
    return jax.shard_map(
        body,
        mesh=mesh,
        in_specs=(
            P("segment", "groups", "gx", "gy", None),
            P("groups", "gx", "gy", None),
            P("segment", "gy", "gx", None, None, None),
            P("segment", None, None),
            P("segment", None),
        ),
        out_specs=(
            P("segment", "groups", "gx", "gy", None),
            P("segment", "gy", "gx", "groups", None, None),
        ),
        check_vma=False,
    )
```
